128 devices in a mesh: dp: 4 (over z_hi, core), ctx: 32 (over z_lo, x, y).
Axes of the slice: x: 4, y: 4, z: 4 (z_hi: 2, z_lo: 2; z = z_hi * 2 + z_lo), core: 2. Of those that a mesh axis runs over, the one named last changes fastest.
Arguments:
- query: bfloat16 [4, 7168, 2560], P('dp', 'ctx'), may hold values from -12 to 12
- keys: bfloat16 [4, 7168, 512], P('dp', 'ctx'), may hold values from -12 to 12
- values: bfloat16 [4, 7168, 512], P('dp', 'ctx'), may hold values from -6 to 6
- section_order: int32 [64], replicated, may hold values from 0 to 63, each once
- kept_sections: int32 [4, 64], P('dp'), may hold values 0 or 1
- segment_ids: int32 [4, 7168], P('dp'), may hold values from 0 to 2, never falling along the last dimension, each value on 1 to 3584 neighbouring positions
- out_weight: bfloat16 [2560, 5120], P('ctx', 'dp'), may hold values from -0.59765625 to 0.59765625
Outputs:
- projected: bfloat16 [4, 7168, 5120], P('dp', 'ctx')
The draws below stay inside these ranges and needn't reach their ends.
All inputs are finite; a program needn't handle non-finite values. No bound on the sum of `kept_sections` on one device may be relied on, other than what follows from the above.
Results may differ from the reference program's by a relative error of at most 0.0085.
Values may be sent and summed in bfloat16 or wider, within the bound.
No kernel may reach another device: no remote copies, remote signals or barrier semaphores. Data moves between devices by JAX's collectives and lax.ppermute only.
A program may use at most 192 MiB of HBM per device.

```python
import math
import jax
import jax.numpy as jnp
import numpy as np
from jax import lax

D = 5120
H = 20
KH = 4
HD = 128
SEC = 112
NSEC = 64
SEQ = 7168
GROUPS = 4


def draw_query(key, part):
    key = jax.random.fold_in(key, 1)
    drawn = jnp.clip(jax.random.normal(key, (GROUPS, SEQ, KH, H // KH, HD), jnp.float32), -6.0, 6.0)
    return drawn.reshape(GROUPS, SEQ, H * HD).astype(jnp.bfloat16)


def draw_keys(key, part):
    key = jax.random.fold_in(key, 3)
    drawn = jnp.clip(jax.random.normal(key, (GROUPS, SEQ, KH, HD), jnp.float32), -6.0, 6.0)
    return drawn.reshape(GROUPS, SEQ, KH * HD).astype(jnp.bfloat16)


def set_ends(array, stream_key, smallest, high):
    index_at = [jax.random.randint(jax.random.fold_in(stream_key, axis), (), 0, length) for axis, length in enumerate(array.shape)]
    main_axis = array.shape.index(max(array.shape))
    next_to = index_at[:main_axis] + [(index_at[main_axis] + 1) % array.shape[main_axis]] + index_at[main_axis + 1:]
    return array.at[tuple(index_at)].set(smallest).at[tuple(next_to)].set(high)


def block_scale(own_key, extent, shards, low, largest):
    level, own = 1.0, jax.random.fold_in(own_key, 6)
    for dim, blocks in shards:
        draws = jnp.exp(jax.random.uniform(jax.random.fold_in(own, dim), (blocks,), jnp.float32, low / len(shards), largest / len(shards)))
        level = level * jnp.repeat(draws, extent[dim] // blocks).reshape([-1 if axis == dim else 1 for axis in range(len(extent))])
    return level


def split_up(amount, total, most, skew):
    loads = [(1 << 20) // math.isqrt(standing ** skew) + 1 for standing in range(2, amount + 1)]
    spare, holding = total - most - (amount - 1), [1] * (amount - 1)
    while spare > 0:
        candidates = [i for i in range(amount - 1) if holding[i] < most]
        whole, left = sum([loads[i] for i in candidates]), spare
        for i in candidates:
            extra = min(most - holding[i], max(1, left * loads[i] // whole), spare)
            holding[i] = holding[i] + extra
            spare = spare - extra
    return np.array([most] + holding)


def uneven(key, number_of, total, reach, slope):
    if number_of == 2:
        one = jax.random.randint(key, (), max(1, total - reach), min(reach, total - 1) + 1)
        return jnp.stack([one, total - one])
    sizes = jnp.asarray(split_up(number_of, total, reach, slope), jnp.int32)
    twos = (number_of - 1) // 2
    giver, receiver = sizes[1:1 + 2 * twos:2], sizes[2:2 + 2 * twos:2]
    margin = jnp.minimum(giver - 1, reach - receiver)
    moved = jax.random.randint(jax.random.fold_in(key, 1), (twos,), 0, 1 << 20) % (margin + 1)
    sizes = sizes.at[1:1 + 2 * twos:2].set(giver - moved).at[2:2 + 2 * twos:2].set(receiver + moved)
    return sizes[jax.random.permutation(jax.random.fold_in(key, 2), number_of)]


def scatter_about(rng, dims, scale, limit, shards=(), held_as=jnp.bfloat16):
    drawn = scale * jax.random.normal(rng, dims, jnp.float32)
    if shards:
        drawn = drawn * block_scale(rng, dims, shards, -0.22, 0.18)
    return jnp.clip(drawn, -limit, limit).astype(held_as)


def setup_inputs(seed: int = 0) -> dict:
    key_of = jax.random.split(jax.random.key(seed), 8)
    return {
        "query": draw_query(jax.random.fold_in(key_of[7], 71), 0),
        "keys": draw_keys(jax.random.fold_in(key_of[7], 71), 0),
        "values": scatter_about(key_of[2], (GROUPS, SEQ, KH * HD), 1.0, 6.0, ((0, 4), (1, 32))),
        "section_order": jax.random.permutation(key_of[3], NSEC).astype(jnp.int32),
        "kept_sections": set_ends((jax.random.randint(key_of[4], (GROUPS, NSEC), 0, 3) < 2).astype(jnp.int32), jax.random.fold_in(key_of[4], 1), 0, 1),
        "segment_ids": jax.vmap(lambda own: jnp.searchsorted(jnp.cumsum(uneven(own, 3, SEQ, SEQ // 2, 0)), jnp.arange(SEQ), side="right"))(jax.random.split(key_of[5], GROUPS)).reshape((GROUPS, SEQ)).astype(jnp.int32),
        "out_weight": scatter_about(key_of[6], (H * HD, D), 0.1, 0.59765625, ((0, 32), (1, 4))),
    }


def positions(section_order):
    layout = jnp.arange(SEQ, dtype=jnp.int32)
    return (section_order[layout // SEC] * SEC + layout % SEC).astype(jnp.int32)

def reference(query, keys, values, section_order, kept_sections, segment_ids, out_weight):
    position = positions(section_order)
    head_groups = H // KH
    score_scale = 1.0 / math.sqrt(HD)
    outputs = []
    for group_index in range(GROUPS):
        q_all = query[group_index].astype(jnp.float32).reshape(SEQ, KH, head_groups, HD)
        k_all = keys[group_index].astype(jnp.float32).reshape(SEQ, KH, HD)
        v_all = values[group_index].astype(jnp.float32).reshape(SEQ, KH, HD)
        segment = segment_ids[group_index][position]
        keep_row = kept_sections[group_index][position // SEC]

        def one_block(block_index):
            start_row = (block_index * SEC).astype(jnp.int32)
            q_block = lax.dynamic_slice_in_dim(q_all, start_row, SEC, 0)
            pos_block = lax.dynamic_slice_in_dim(position, start_row, SEC, 0)
            seg_block = lax.dynamic_slice_in_dim(segment, start_row, SEC, 0)
            scores = jnp.einsum('tkgd,skd->kgts', q_block, k_all) * score_scale
            visible = (position[None, :] <= pos_block[:, None]) & (segment[None, :] == seg_block[:, None])
            scores = jnp.where(visible, scores, -1e+30)
            peak = lax.optimization_barrier(jnp.max(scores, axis=-1, keepdims=True))
            weights = jnp.where(visible, jnp.exp(scores - peak), 0.0).astype(jnp.bfloat16)
            weights = lax.optimization_barrier(weights).astype(jnp.float32)
            denominator = lax.optimization_barrier(jnp.sum(weights, axis=-1))
            numerator = jnp.einsum('kgts,skd->kgtd', weights, v_all)
            return jnp.transpose(numerator / denominator[..., None], (2, 0, 1, 3)).reshape(SEC, H * HD)
        attended = lax.map(one_block, jnp.arange(SEQ // SEC, dtype=jnp.int32)).reshape(SEQ, H * HD)
        attended = (attended * keep_row[:, None].astype(jnp.float32)).astype(jnp.bfloat16)
        outputs.append(jnp.dot(attended, out_weight, preferred_element_type=jnp.float32).astype(jnp.bfloat16))
    return jnp.stack(outputs)
```

```python
import functools
import math

import jax
import jax.numpy as jnp
from jax import lax
from jax.experimental import pallas as pl
from jax.experimental.pallas import tpu as pltpu
from jax.sharding import Mesh, PartitionSpec as P

HD = 128
RING = 4
SHIFTS = (0, -1, 1, 2)
BLOCK_KEYS = 512
ROW_TILE = 16
Z = ("zh", "zl")


def shifted(array, axis, step, size=RING):
    return lax.ppermute(array, axis, [(i, (i + step) % size) for i in range(size)])


def ring_gather(array):
    def on(axis):
        half = array.shape[0] // 2
        from_left = shifted(array, axis, 1)
        from_right = shifted(array, axis, -1)
        far_head = shifted(from_left[:half], axis, 1)
        far_tail = shifted(from_right[half:], axis, -1)
        return array, from_left, from_right, far_head, far_tail

    return on


def direct_gather(array, axis):
    return jnp.stack([array] + [shifted(array, axis, -s) for s in SHIFTS[1:]])


def wrap(value):
    return lax.rem(value + RING, RING)


def attention_kernel(
    groups, sec, nsec, max_range, coords, order, kept, starts, *refs
):
    q_refs, kv_refs, out_refs = refs[:4], refs[4:14], refs[14:18]
    k_all, v_all, scores, acc, peak, sem = refs[18:]
    zl, x, y = coords[0], coords[1], coords[2]
    rows = nsec * sec
    factor = math.log2(math.e) / math.sqrt(HD)
    q_rows = groups * sec

    def copies(act):
        for side in range(2):
            own_zl = zl if side == 0 else 1 - zl
            base = side * 5
            for x_rel in range(4):
                abs_x = wrap(x + SHIFTS[x_rel])
                for y_rel in range(4):
                    abs_y = wrap(y + SHIFTS[y_rel])
                    if x_rel < 3:
                        source = kv_refs[base + x_rel].at[y_rel]
                    else:
                        source = kv_refs[base + 3 + y_rel // 2].at[y_rel % 2]
                    for part in range(2):
                        section = ((own_zl * RING + abs_x) * RING + abs_y) * 2 + part
                        at = pl.multiple_of(order[section] * sec, ROW_TILE)
                        act(source.at[pl.ds(part * sec, sec), pl.ds(0, HD)], k_all.at[pl.ds(at, sec), :])
                        act(source.at[pl.ds(part * sec, sec), pl.ds(HD, HD)], v_all.at[pl.ds(at, sec), pl.ds(0, HD)])

    copies(lambda a, b: pltpu.make_async_copy(a, b, sem).start())
    pad = k_all.shape[0] - rows
    k_all[pl.ds(rows, pad), :] = jnp.zeros((pad, HD), k_all.dtype)
    v_all[pl.ds(rows, pad), pl.ds(0, HD)] = jnp.zeros((pad, HD), v_all.dtype)
    v_all[:, pl.ds(HD, HD)] = jnp.ones((k_all.shape[0], HD), v_all.dtype)
    copies(lambda a, b: pltpu.make_async_copy(a, b, sem).wait())

    first, second = starts[0], starts[1]

    def segment_start(pos):
        return jnp.where(pos >= second, second, jnp.where(pos >= first, first, 0))

    for piece in range(4):
        abs_y = wrap(y + SHIFTS[piece])
        q_ref, out_ref = q_refs[piece], out_refs[piece]

        def one_section(part, _, q_ref=q_ref, out_ref=out_ref, abs_y=abs_y):
            section = ((zl * RING + x) * RING + abs_y) * 2 + part
            place = order[section]
            begin = place * sec
            own_rows = pl.ds(pl.multiple_of(part * sec, ROW_TILE), sec)

            @pl.when(kept[place] == 0)
            def _():
                out_ref[own_rows, :] = jnp.zeros((sec, groups * HD), out_ref.dtype)

            @pl.when(kept[place] != 0)
            def _():
                key_first = segment_start(begin) // ROW_TILE * ROW_TILE
                last_start = segment_start(begin + sec - 1)
                blocks = (begin + sec - key_first + BLOCK_KEYS - 1) // BLOCK_KEYS
                q_tile = jnp.concatenate(
                    [q_ref[own_rows, pl.ds(g * HD, HD)] for g in range(groups)], axis=0
                )
                peak[...] = jnp.full(peak.shape, -1e30, jnp.float32)

                def lane_max(block_scores):
                    best = peak[...]
                    for i in range(BLOCK_KEYS // HD):
                        best = jnp.maximum(best, block_scores[:, i * HD : (i + 1) * HD])
                    peak[...] = best

                def score(block, _):
                    at = pl.multiple_of(key_first + block * BLOCK_KEYS, ROW_TILE)
                    raw = lax.dot_general(
                        q_tile,
                        k_all[pl.ds(at, BLOCK_KEYS), :],
                        (((1,), (1,)), ((), ())),
                        preferred_element_type=jnp.float32,
                    )
                    masked = (at < last_start) | (at + BLOCK_KEYS > begin)

                    @pl.when(masked)
                    def _():
                        row_pos = begin + lax.rem(
                            lax.broadcasted_iota(jnp.int32, (q_rows, 1), 0), sec
                        )
                        row_start = segment_start(row_pos)
                        key_pos = at + lax.broadcasted_iota(jnp.int32, (1, BLOCK_KEYS), 1)
                        seen = (key_pos <= row_pos) & (key_pos >= row_start)
                        hidden = jnp.where(seen, raw, -1e30)
                        scores[block] = hidden
                        lane_max(hidden)

                    @pl.when(jnp.logical_not(masked))
                    def _():
                        scores[block] = raw
                        lane_max(raw)

                    return 0

                lax.fori_loop(0, blocks, score, 0)
                top = jnp.max(peak[...], axis=1, keepdims=True) * factor
                acc[...] = jnp.zeros(acc.shape, jnp.float32)

                def weigh(block, _):
                    at = pl.multiple_of(key_first + block * BLOCK_KEYS, ROW_TILE)
                    weights = jnp.exp2(scores[block] * factor - top).astype(jnp.bfloat16)
                    acc[...] += jnp.dot(
                        weights,
                        v_all[pl.ds(at, BLOCK_KEYS), :],
                        preferred_element_type=jnp.float32,
                    )
                    return 0

                lax.fori_loop(0, blocks, weigh, 0)
                result = (acc[:, pl.ds(0, HD)] / acc[:, pl.ds(HD, HD)]).astype(out_ref.dtype)
                for g in range(groups):
                    out_ref[own_rows, pl.ds(g * HD, HD)] = result[g * sec : (g + 1) * sec]

            return 0

        lax.fori_loop(0, 2, one_section, 0)


def attention(coords, order, kept, starts, q_pieces, kv_pieces, sec, nsec):
    groups = q_pieces[0].shape[1] // HD
    rows = nsec * sec
    max_range = rows // 2 + sec + ROW_TILE
    max_blocks = -(-max_range // BLOCK_KEYS)
    smem = pl.BlockSpec(memory_space=pltpu.SMEM)
    vmem = pl.BlockSpec(memory_space=pltpu.VMEM)
    return pl.pallas_call(
        functools.partial(attention_kernel, groups, sec, nsec, max_range),
        out_shape=[jax.ShapeDtypeStruct(q.shape, q.dtype) for q in q_pieces],
        in_specs=[smem] * 4 + [vmem] * 4 + [pl.BlockSpec(memory_space=pl.ANY)] * 10,
        out_specs=[vmem] * 4,
        scratch_shapes=[
            pltpu.VMEM((rows + BLOCK_KEYS, HD), jnp.bfloat16),
            pltpu.VMEM((rows + BLOCK_KEYS, 2 * HD), jnp.bfloat16),
            pltpu.VMEM((max_blocks, groups * sec, BLOCK_KEYS), jnp.float32),
            pltpu.VMEM((groups * sec, 2 * HD), jnp.float32),
            pltpu.VMEM((groups * sec, HD), jnp.float32),
            pltpu.SemaphoreType.DMA,
        ],
        compiler_params=pltpu.CompilerParams(vmem_limit_bytes=48 * 2**20),
        cost_estimate=pl.CostEstimate(
            flops=8 * 10**9, bytes_accessed=6 * 10**6, transcendentals=16 * 10**6
        ),
        name="attend",
    )(coords, order, kept, starts, *q_pieces, *kv_pieces)


AXIS_ORDERS = (("x", "y", "z"), ("y", "z", "x"), ("z", "x", "y"))


def project_kernel(depth, cols, parts, coords, *refs):
    att_refs, weight_refs = refs[:8], refs[8:23]
    own_out, other_out = refs[23:25]
    att, weights, sems = refs[25], refs[26:29], refs[29]
    place = {"z": coords[3], "x": coords[1], "y": coords[2]}
    offsets = (0, parts[0], parts[0] + parts[1])

    def copies(k, act):
        axes = AXIS_ORDERS[k]

        def first_axis(i, _):
            shift_i = jnp.where(i == 0, 0, jnp.where(i == 1, -1, jnp.where(i == 2, 1, 2)))
            for j in range(4):
                for last in range(4):
                    at = {
                        axes[0]: wrap(place[axes[0]] + shift_i),
                        axes[1]: wrap(place[axes[1]] + SHIFTS[j]),
                        axes[2]: wrap(place[axes[2]] + SHIFTS[last]),
                    }
                    z_hi, z_lo = at["z"] // 2, lax.rem(at["z"], 2)
                    row = pl.multiple_of(
                        ((z_lo * RING + at["x"]) * RING + at["y"]) * depth, ROW_TILE
                    )
                    col = pl.multiple_of(z_hi * parts[k], HD)
                    if last < 3:
                        source = weight_refs[5 * k + last].at[j, i]
                    else:
                        source = weight_refs[5 * k + 3 + j // 2].at[j % 2, i]
                    act(source, weights[k].at[pl.ds(row, depth), pl.ds(col, parts[k])], sems.at[k])
            return 0

        lax.fori_loop(0, 4, first_axis, 0)

    for k in range(3):
        copies(k, lambda a, b, s: pltpu.make_async_copy(a, b, s).start())
    tok = own_out.shape[0]
    wide = att_refs[0].shape[1]
    for who in range(2):
        for j in range(4):
            head = wrap(coords[2] + SHIFTS[j])
            att[pl.ds(who * tok, tok), pl.ds(pl.multiple_of(head * wide, HD), wide)] = att_refs[
                4 * who + j
            ][...]
    for k in range(3):
        copies(k, lambda a, b, s: pltpu.make_async_copy(a, b, s).wait())
        for z_hi in range(2):
            got = jnp.dot(
                att[...],
                weights[k][:, pl.ds(z_hi * parts[k], parts[k])],
                preferred_element_type=jnp.float32,
            ).astype(own_out.dtype)
            at = pl.ds(z_hi * cols + offsets[k], parts[k])
            own_out[:, at] = got[:tok]
            other_out[:, at] = got[tok:]


def project(coords, own_att, other_att, weight_pieces, depth, cols, parts):
    tok = own_att[0].shape[0]
    wide = own_att[0].shape[1]
    out = jax.ShapeDtypeStruct((tok, 2 * cols), jnp.bfloat16)
    vmem = pl.BlockSpec(memory_space=pltpu.VMEM)
    return pl.pallas_call(
        functools.partial(project_kernel, depth, cols, parts),
        out_shape=[out, out],
        in_specs=[pl.BlockSpec(memory_space=pltpu.SMEM)]
        + [vmem] * 8
        + [pl.BlockSpec(memory_space=pl.ANY)] * 15,
        out_specs=[vmem] * 2,
        scratch_shapes=[pltpu.VMEM((2 * tok, 4 * wide), jnp.bfloat16)]
        + [pltpu.VMEM((4 * wide, 2 * part), jnp.bfloat16) for part in parts]
        + [pltpu.SemaphoreType.DMA((3,))],
        compiler_params=pltpu.CompilerParams(vmem_limit_bytes=48 * 2**20),
        cost_estimate=pl.CostEstimate(
            flops=6 * 10**9, bytes_accessed=18 * 10**6, transcendentals=0
        ),
        name="project",
    )(coords, *own_att, *other_att, *weight_pieces)


def per_device(query, keys, values, section_order, kept_sections, segment_ids, out_weight):
    tok = query.shape[1]
    sec = tok // 2
    nsec = section_order.shape[0]
    zh, core = lax.axis_index("zh"), lax.axis_index("c")
    zl, x, y = lax.axis_index("zl"), lax.axis_index("x"), lax.axis_index("y")
    coords = jnp.stack([zl, x, y, zh * 2 + zl]).astype(jnp.int32)
    starts = jnp.stack([jnp.sum(segment_ids[0] < 1), jnp.sum(segment_ids[0] < 2)]).astype(jnp.int32)

    def head_slice(array, shift):
        wide = array.shape[2] // RING
        return lax.dynamic_slice_in_dim(array[0], wrap(y + shift) * wide, wide, 1)

    kv_pieces, q_pieces = [], []
    for shift in SHIFTS:
        kv = jnp.concatenate([head_slice(keys, -shift), head_slice(values, -shift)], axis=1)
        kv_pieces.append(kv if shift == 0 else shifted(kv, "y", -shift))
    for shift in SHIFTS:
        q = head_slice(query, -shift)
        q_pieces.append(q if shift == 0 else shifted(q, "y", -shift))
    near = jnp.stack(kv_pieces)
    far = shifted(near, "zl", 1, 2)
    kv_all = ring_gather(near)("x") + ring_gather(far)("x")

    depth, cols = out_weight.shape
    tiles = cols // HD
    third = tiles // 3
    parts = ((tiles - 2 * third) * HD, third * HD, third * HD)
    names = {"x": "x", "y": "y", "z": Z}
    weight_pieces, at = [], 0
    for k in range(3):
        part = out_weight[:, at : at + parts[k]]
        at += parts[k]
        axes = [names[a] for a in AXIS_ORDERS[k]]
        square = direct_gather(direct_gather(part, axes[0]), axes[1])
        weight_pieces += ring_gather(square)(axes[2])

    attended = attention(
        coords, section_order, kept_sections[0], starts, q_pieces, kv_all, sec, nsec
    )
    by_shift = dict(zip(SHIFTS, attended))
    back = {0: by_shift[0]}
    for shift in SHIFTS[1:]:
        back[wrap_static(-shift)] = shifted(by_shift[shift], "y", shift)
    own_att = [back[s] for s in SHIFTS]
    other_att = [shifted(a, "c", 1, 2) for a in own_att]
    own_out, other_out = project(coords, own_att, other_att, weight_pieces, depth, cols, parts)
    mine = own_out.reshape(tok, 2, 1, cols)
    theirs = shifted(other_out, "c", 1, 2).reshape(tok, 2, 1, cols)
    low = core == 0
    both = jnp.concatenate(
        [jnp.where(low, mine, theirs), jnp.where(low, theirs, mine)], axis=2
    )
    return both.reshape(1, tok, 4 * cols)


def wrap_static(shift):
    return 2 if shift in (2, -2) else shift


def solution(mesh):
    fine = Mesh(mesh.devices.reshape(2, 2, 2, 4, 4), ("zh", "c", "zl", "x", "y"))
    dp, ctx = ("zh", "c"), ("zl", "x", "y")
    return jax.shard_map(
        per_device,
        mesh=fine,
        in_specs=(
            P(dp, ctx, None),
            P(dp, ctx, None),
            P(dp, ctx, None),
            P(),
            P(dp, None),
            P(dp, None),
            P(ctx, dp),
        ),
        out_specs=P(dp, ctx, None),
        check_vma=False,
    )
```

```python
import functools
import math

import jax
import jax.numpy as jnp
from jax import lax
from jax.experimental import pallas as pl
from jax.experimental.pallas import tpu as pltpu
from jax.sharding import Mesh, PartitionSpec as P

HD = 128
RING = 4
SHIFTS = (0, -1, 1, 2)
BLOCK_KEYS = 512
ROW_TILE = 16


def shifted(array, axis, step, size=RING):
    return lax.ppermute(array, axis, [(i, (i + step) % size) for i in range(size)])


def ring_gather(array):
    def on(axis):
        half = array.shape[0] // 2
        from_left = shifted(array, axis, 1)
        from_right = shifted(array, axis, -1)
        far_head = shifted(from_left[:half], axis, 1)
        far_tail = shifted(from_right[half:], axis, -1)
        return array, from_left, from_right, far_head, far_tail

    return on


def wrap(value):
    return lax.rem(value + RING, RING)


def attention_kernel(
    groups, sec, nsec, max_range, coords, order, kept, starts, *refs
):
    q_refs, kv_refs, out_refs = refs[:4], refs[4:14], refs[14:18]
    k_all, v_all, scores, acc, peak, sem = refs[18:]
    zl, x, y = coords[0], coords[1], coords[2]
    rows = nsec * sec
    factor = math.log2(math.e) / math.sqrt(HD)
    q_rows = groups * sec

    def copies(act):
        for side in range(2):
            own_zl = zl if side == 0 else 1 - zl
            base = side * 5
            for x_rel in range(4):
                abs_x = wrap(x + SHIFTS[x_rel])
                for y_rel in range(4):
                    abs_y = wrap(y + SHIFTS[y_rel])
                    if x_rel < 3:
                        source = kv_refs[base + x_rel].at[y_rel]
                    else:
                        source = kv_refs[base + 3 + y_rel // 2].at[y_rel % 2]
                    for part in range(2):
                        section = ((own_zl * RING + abs_x) * RING + abs_y) * 2 + part
                        at = pl.multiple_of(order[section] * sec, ROW_TILE)
                        act(source.at[pl.ds(part * sec, sec), pl.ds(0, HD)], k_all.at[pl.ds(at, sec), :])
                        act(source.at[pl.ds(part * sec, sec), pl.ds(HD, HD)], v_all.at[pl.ds(at, sec), pl.ds(0, HD)])

    copies(lambda a, b: pltpu.make_async_copy(a, b, sem).start())
    pad = k_all.shape[0] - rows
    k_all[pl.ds(rows, pad), :] = jnp.zeros((pad, HD), k_all.dtype)
    v_all[pl.ds(rows, pad), pl.ds(0, HD)] = jnp.zeros((pad, HD), v_all.dtype)
    v_all[:, pl.ds(HD, HD)] = jnp.ones((k_all.shape[0], HD), v_all.dtype)
    copies(lambda a, b: pltpu.make_async_copy(a, b, sem).wait())

    first, second = starts[0], starts[1]

    def segment_start(pos):
        return jnp.where(pos >= second, second, jnp.where(pos >= first, first, 0))

    for piece in range(4):
        abs_y = wrap(y + SHIFTS[piece])
        q_ref, out_ref = q_refs[piece], out_refs[piece]

        def one_section(part, _, q_ref=q_ref, out_ref=out_ref, abs_y=abs_y):
            section = ((zl * RING + x) * RING + abs_y) * 2 + part
            place = order[section]
            begin = place * sec
            own_rows = pl.ds(pl.multiple_of(part * sec, ROW_TILE), sec)

            @pl.when(kept[place] == 0)
            def _():
                out_ref[own_rows, :] = jnp.zeros((sec, groups * HD), out_ref.dtype)

            @pl.when(kept[place] != 0)
            def _():
                key_first = segment_start(begin) // ROW_TILE * ROW_TILE
                last_start = segment_start(begin + sec - 1)
                blocks = (begin + sec - key_first + BLOCK_KEYS - 1) // BLOCK_KEYS
                q_tile = jnp.concatenate(
                    [q_ref[own_rows, pl.ds(g * HD, HD)] for g in range(groups)], axis=0
                )
                peak[...] = jnp.full(peak.shape, -1e30, jnp.float32)

                def lane_max(block_scores):
                    best = peak[...]
                    for i in range(BLOCK_KEYS // HD):
                        best = jnp.maximum(best, block_scores[:, i * HD : (i + 1) * HD])
                    peak[...] = best

                def score(block, _):
                    at = pl.multiple_of(key_first + block * BLOCK_KEYS, ROW_TILE)
                    raw = lax.dot_general(
                        q_tile,
                        k_all[pl.ds(at, BLOCK_KEYS), :],
                        (((1,), (1,)), ((), ())),
                        preferred_element_type=jnp.float32,
                    )
                    masked = (at < last_start) | (at + BLOCK_KEYS > begin)

                    @pl.when(masked)
                    def _():
                        row_pos = begin + lax.rem(
                            lax.broadcasted_iota(jnp.int32, (q_rows, 1), 0), sec
                        )
                        row_start = segment_start(row_pos)
                        key_pos = at + lax.broadcasted_iota(jnp.int32, (1, BLOCK_KEYS), 1)
                        seen = (key_pos <= row_pos) & (key_pos >= row_start)
                        hidden = jnp.where(seen, raw, -1e30)
                        scores[block] = hidden
                        lane_max(hidden)

                    @pl.when(jnp.logical_not(masked))
                    def _():
                        scores[block] = raw
                        lane_max(raw)

                    return 0

                lax.fori_loop(0, blocks, score, 0)
                top = jnp.max(peak[...], axis=1, keepdims=True) * factor
                acc[...] = jnp.zeros(acc.shape, jnp.float32)

                def weigh(block, _):
                    at = pl.multiple_of(key_first + block * BLOCK_KEYS, ROW_TILE)
                    weights = jnp.exp2(scores[block] * factor - top).astype(jnp.bfloat16)
                    acc[...] += jnp.dot(
                        weights,
                        v_all[pl.ds(at, BLOCK_KEYS), :],
                        preferred_element_type=jnp.float32,
                    )
                    return 0

                lax.fori_loop(0, blocks, weigh, 0)
                result = (acc[:, pl.ds(0, HD)] / acc[:, pl.ds(HD, HD)]).astype(out_ref.dtype)
                for g in range(groups):
                    out_ref[own_rows, pl.ds(g * HD, HD)] = result[g * sec : (g + 1) * sec]

            return 0

        lax.fori_loop(0, 2, one_section, 0)


def attention(coords, order, kept, starts, q_pieces, kv_pieces, sec, nsec):
    groups = q_pieces[0].shape[1] // HD
    rows = nsec * sec
    max_range = rows // 2 + sec + ROW_TILE
    max_blocks = -(-max_range // BLOCK_KEYS)
    smem = pl.BlockSpec(memory_space=pltpu.SMEM)
    vmem = pl.BlockSpec(memory_space=pltpu.VMEM)
    return pl.pallas_call(
        functools.partial(attention_kernel, groups, sec, nsec, max_range),
        out_shape=[jax.ShapeDtypeStruct(q.shape, q.dtype) for q in q_pieces],
        in_specs=[smem] * 4 + [vmem] * 4 + [pl.BlockSpec(memory_space=pl.ANY)] * 10,
        out_specs=[vmem] * 4,
        scratch_shapes=[
            pltpu.VMEM((rows + BLOCK_KEYS, HD), jnp.bfloat16),
            pltpu.VMEM((rows + BLOCK_KEYS, 2 * HD), jnp.bfloat16),
            pltpu.VMEM((max_blocks, groups * sec, BLOCK_KEYS), jnp.float32),
            pltpu.VMEM((groups * sec, 2 * HD), jnp.float32),
            pltpu.VMEM((groups * sec, HD), jnp.float32),
            pltpu.SemaphoreType.DMA,
        ],
        compiler_params=pltpu.CompilerParams(vmem_limit_bytes=48 * 2**20),
        cost_estimate=pl.CostEstimate(
            flops=8 * 10**9, bytes_accessed=6 * 10**6, transcendentals=16 * 10**6
        ),
        name="attend",
    )(coords, order, kept, starts, *q_pieces, *kv_pieces)


def project_kernel(coords, core, *refs):
    att_refs, weights = refs[:8], refs[8]
    own_out, other_out, att = refs[9:]
    tok, wide = att_refs[0].shape

    @pl.when(pl.program_id(0) == 0)
    def _():
        for who in range(2):
            for j in range(4):
                head = wrap(coords[2] + SHIFTS[j])
                at = pl.multiple_of(head * wide, HD)
                att[pl.ds(who * tok, tok), pl.ds(at, wide)] = att_refs[4 * who + j][...]

    got = jnp.dot(att[...], weights[...], preferred_element_type=jnp.float32)
    got = got.astype(own_out.dtype)
    own_out[...] = got[:tok]
    other_out[...] = got[tok:]


def project(coords, core, own_att, other_att, weights, cols):
    tok, wide = own_att[0].shape
    rows = RING * wide
    split = 2
    step = cols // split
    piece = pl.BlockSpec((tok, wide), lambda i, *_: (0, 0))
    return pl.pallas_call(
        project_kernel,
        out_shape=[
            jax.ShapeDtypeStruct((tok, 4 * cols), jnp.bfloat16),
            jax.ShapeDtypeStruct((tok, 2 * cols), jnp.bfloat16),
        ],
        grid_spec=pltpu.PrefetchScalarGridSpec(
            num_scalar_prefetch=2,
            grid=(2 * split,),
            in_specs=[piece] * 8
            + [pl.BlockSpec((rows, step), lambda i, *_: (i // split, i % split))],
            out_specs=[
                pl.BlockSpec(
                    (tok, step),
                    lambda i, where, core: (0, (i // split * 2 + core[0]) * split + i % split),
                ),
                pl.BlockSpec((tok, step), lambda i, *_: (0, i)),
            ],
            scratch_shapes=[pltpu.VMEM((2 * tok, rows), jnp.bfloat16)],
        ),
        compiler_params=pltpu.CompilerParams(vmem_limit_bytes=48 * 2**20),
        cost_estimate=pl.CostEstimate(
            flops=6 * 10**9, bytes_accessed=18 * 10**6, transcendentals=0
        ),
        name="project",
    )(coords, core, *own_att, *other_att, weights)


def merge_kernel(core, whole, theirs, out):
    del core, whole
    out[...] = theirs[...]


def merge(core, whole, theirs, cols):
    tok = theirs.shape[0]
    return pl.pallas_call(
        merge_kernel,
        out_shape=jax.ShapeDtypeStruct(whole.shape, whole.dtype),
        grid_spec=pltpu.PrefetchScalarGridSpec(
            num_scalar_prefetch=1,
            grid=(2,),
            in_specs=[
                pl.BlockSpec(memory_space=pl.ANY),
                pl.BlockSpec((tok, cols), lambda i, core: (0, i)),
            ],
            out_specs=pl.BlockSpec((tok, cols), lambda i, core: (0, i * 2 + 1 - core[0])),
        ),
        input_output_aliases={1: 0},
        cost_estimate=pl.CostEstimate(flops=0, bytes_accessed=3 * 10**6, transcendentals=0),
        name="merge",
    )(core, whole, theirs)


def per_device(query, keys, values, section_order, kept_sections, segment_ids, out_weight):
    tok = query.shape[1]
    sec = tok // 2
    nsec = section_order.shape[0]
    core = lax.axis_index("c")
    zl, x, y = lax.axis_index("zl"), lax.axis_index("x"), lax.axis_index("y")
    coords = jnp.stack([zl, x, y]).astype(jnp.int32)
    starts = jnp.stack([jnp.sum(segment_ids[0] < 1), jnp.sum(segment_ids[0] < 2)]).astype(jnp.int32)

    def head_slice(array, shift):
        wide = array.shape[2] // RING
        return lax.dynamic_slice_in_dim(array[0], wrap(y + shift) * wide, wide, 1)

    kv_pieces, q_pieces = [], []
    for shift in SHIFTS:
        kv = jnp.concatenate([head_slice(keys, -shift), head_slice(values, -shift)], axis=1)
        kv_pieces.append(kv if shift == 0 else shifted(kv, "y", -shift))
    for shift in SHIFTS:
        q = head_slice(query, -shift)
        q_pieces.append(q if shift == 0 else shifted(q, "y", -shift))
    near = jnp.stack(kv_pieces)
    far = shifted(near, "zl", 1, 2)
    kv_all = ring_gather(near)("x") + ring_gather(far)("x")

    cols = out_weight.shape[1]
    weights = lax.all_gather(out_weight, ("zh", "zl", "x", "y"), axis=0, tiled=True)

    attended = attention(
        coords, section_order, kept_sections[0], starts, q_pieces, kv_all, sec, nsec
    )
    by_shift = dict(zip(SHIFTS, attended))
    back = {0: by_shift[0]}
    for shift in SHIFTS[1:]:
        back[wrap_static(-shift)] = shifted(by_shift[shift], "y", shift)
    own_att = [back[s] for s in SHIFTS]
    other_att = [shifted(a, "c", 1, 2) for a in own_att]
    which = core[None].astype(jnp.int32)
    whole, for_other = project(coords, which, own_att, other_att, weights, cols)
    return merge(which, whole, shifted(for_other, "c", 1, 2), cols)[None]


def wrap_static(shift):
    return 2 if shift in (2, -2) else shift


def solution(mesh):
    fine = Mesh(mesh.devices.reshape(2, 2, 2, 4, 4), ("zh", "c", "zl", "x", "y"))
    dp, ctx = ("zh", "c"), ("zl", "x", "y")
    return jax.shard_map(
        per_device,
        mesh=fine,
        in_specs=(
            P(dp, ctx, None),
            P(dp, ctx, None),
            P(dp, ctx, None),
            P(),
            P(dp, None),
            P(dp, None),
            P(ctx, dp),
        ),
        out_specs=P(dp, ctx, None),
        check_vma=False,
    )
```

```python
import functools
import math

import jax
import jax.numpy as jnp
from jax import lax
from jax.experimental import pallas as pl
from jax.experimental.pallas import tpu as pltpu
from jax.sharding import Mesh, PartitionSpec as P

HD = 128
RING = 4
SHIFTS = (0, -1, 1, 2)
BLOCK_KEYS = 2048
TAIL_STEP = 256
ROW_TILE = 16


def shifted(array, axis, step, size=RING):
    return lax.ppermute(array, axis, [(i, (i + step) % size) for i in range(size)])


def ring_gather(array):
    def on(axis):
        half = array.shape[0] // 2
        from_left = shifted(array, axis, 1)
        from_right = shifted(array, axis, -1)
        far_head = shifted(from_left[:half], axis, 1)
        far_tail = shifted(from_right[half:], axis, -1)
        return array, from_left, from_right, far_head, far_tail

    return on


def wrap(value):
    return lax.rem(value + RING, RING)


def attention_kernel(
    groups, sec, nsec, coords, order, kept, starts, *refs
):
    q_refs, kv_refs, out_refs = refs[:4], refs[4:14], refs[14:18]
    held, q_all, out_all, acc, peak, sem = refs[18:]
    zl, x, y = coords[0], coords[1], coords[2]
    rows = nsec * sec
    factor = math.log2(math.e) / math.sqrt(HD)

    def copies(act):
        for side in range(2):
            own_zl = zl if side == 0 else 1 - zl
            base = side * 5
            for x_rel in range(4):
                abs_x = wrap(x + SHIFTS[x_rel])
                for y_rel in range(4):
                    abs_y = wrap(y + SHIFTS[y_rel])
                    if x_rel < 3:
                        source = kv_refs[base + x_rel].at[y_rel]
                    else:
                        source = kv_refs[base + 3 + y_rel // 2].at[y_rel % 2]
                    for part in range(2):
                        section = ((own_zl * RING + abs_x) * RING + abs_y) * 2 + part
                        at = pl.multiple_of(order[section] * sec, ROW_TILE)
                        act(
                            source.at[pl.ds(part * sec, sec), :],
                            held.at[pl.ds(at, sec), pl.ds(0, 2 * HD)],
                        )

    copies(lambda a, b: pltpu.make_async_copy(a, b, sem).start())
    pad = held.shape[0] - rows
    held[pl.ds(rows, pad), pl.ds(0, 2 * HD)] = jnp.zeros((pad, 2 * HD), held.dtype)
    held[:, pl.ds(2 * HD, HD)] = jnp.ones((held.shape[0], HD), held.dtype)
    copies(lambda a, b: pltpu.make_async_copy(a, b, sem).wait())

    first, second = starts[0], starts[1]

    def segment_start(pos):
        return jnp.where(pos >= second, second, jnp.where(pos >= first, first, 0))

    for piece in range(4):
        q_all[pl.ds(piece * 2 * sec, 2 * sec), :] = q_refs[piece][...]

    def one_section(index, _):
        piece, part = index // 2, lax.rem(index, 2)
        shift = jnp.where(piece == 1, -1, jnp.where(piece == 0, 0, piece - 1))
        section = ((zl * RING + x) * RING + wrap(y + shift)) * 2 + part
        place = order[section]
        begin = place * sec
        own_rows = pl.ds(pl.multiple_of(index * sec, ROW_TILE), sec)

        @pl.when(kept[place] == 0)
        def _():
            out_all[own_rows, :] = jnp.zeros((sec, groups * HD), out_all.dtype)

        @pl.when(kept[place] != 0)
        def _():
            key_first = segment_start(begin) // ROW_TILE * ROW_TILE
            last_start = segment_start(begin + sec - 1)
            full = (begin + sec - key_first) // BLOCK_KEYS
            tail_first = key_first + full * BLOCK_KEYS
            tail_steps = (begin + sec - tail_first + TAIL_STEP - 1) // TAIL_STEP
            peak[...] = jnp.full(peak.shape, -1e30, jnp.float32)
            acc[...] = jnp.zeros(acc.shape, jnp.float32)

            def step(first, width, masked):
                at = pl.multiple_of(first, ROW_TILE)
                keys = held[pl.ds(at, width), pl.ds(0, HD)]
                values = held[pl.ds(at, width), pl.ds(HD, 2 * HD)]
                if masked:
                    row_pos = begin + lax.broadcasted_iota(jnp.int32, (sec, 1), 0)
                    row_start = segment_start(row_pos)
                    key_pos = at + lax.broadcasted_iota(jnp.int32, (1, width), 1)
                    seen = (key_pos <= row_pos) & (key_pos >= row_start)
                def score(g):
                    got = lax.dot_general(
                        q_all[own_rows, pl.ds(g * HD, HD)],
                        keys,
                        (((1,), (1,)), ((), ())),
                        preferred_element_type=jnp.float32,
                    )
                    return jnp.where(seen, got, -1e30) if masked else got

                def weigh(g, got):
                    rows_g = pl.ds(g * sec, sec)
                    before = peak[rows_g, :]
                    top = jnp.maximum(before, jnp.max(got, axis=1, keepdims=True))
                    peak[rows_g, :] = top
                    scaled = top * factor
                    weights = jnp.exp2(
                        got * factor - jnp.concatenate([scaled] * (width // HD), axis=1)
                    ).astype(jnp.bfloat16)
                    return weights, jnp.exp2(before * factor - scaled)

                def add(g, weights, rescale):
                    rows_g = pl.ds(g * sec, sec)
                    acc[rows_g, :] = acc[rows_g, :] * jnp.concatenate(
                        [rescale, rescale], axis=1
                    ) + jnp.dot(weights, values, preferred_element_type=jnp.float32)

                ahead = score(0)
                waiting = None
                for g in range(groups):
                    got, ahead = ahead, score(g + 1) if g + 1 < groups else None
                    if waiting is not None:
                        add(g - 1, *waiting)
                    waiting = weigh(g, got)
                add(groups - 1, *waiting)

            def full_block(block, _):
                first = key_first + block * BLOCK_KEYS
                masked = (first < last_start) | (first + BLOCK_KEYS > begin)
                pl.when(masked)(lambda: step(first, BLOCK_KEYS, True))
                pl.when(jnp.logical_not(masked))(lambda: step(first, BLOCK_KEYS, False))
                return 0

            lax.fori_loop(0, full, full_block, 0)
            for steps in range(1, BLOCK_KEYS // TAIL_STEP + 1):
                pl.when(tail_steps == steps)(
                    lambda steps=steps: step(tail_first, steps * TAIL_STEP, True)
                )
            for g in range(groups):
                rows_g = pl.ds(g * sec, sec)
                out_all[own_rows, pl.ds(g * HD, HD)] = (
                    acc[rows_g, pl.ds(0, HD)] / acc[rows_g, pl.ds(HD, HD)]
                ).astype(out_all.dtype)

        return 0

    lax.fori_loop(0, 8, one_section, 0)
    for piece in range(4):
        out_refs[piece][...] = out_all[pl.ds(piece * 2 * sec, 2 * sec), :]


def attention(coords, order, kept, starts, q_pieces, kv_pieces, sec, nsec):
    groups = q_pieces[0].shape[1] // HD
    rows = nsec * sec
    smem = pl.BlockSpec(memory_space=pltpu.SMEM)
    vmem = pl.BlockSpec(memory_space=pltpu.VMEM)
    return pl.pallas_call(
        functools.partial(attention_kernel, groups, sec, nsec),
        out_shape=[jax.ShapeDtypeStruct(q.shape, q.dtype) for q in q_pieces],
        in_specs=[smem] * 4 + [vmem] * 4 + [pl.BlockSpec(memory_space=pl.ANY)] * 10,
        out_specs=[vmem] * 4,
        scratch_shapes=[
            pltpu.VMEM((rows + TAIL_STEP, 3 * HD), jnp.bfloat16),
            pltpu.VMEM((8 * sec, groups * HD), jnp.bfloat16),
            pltpu.VMEM((8 * sec, groups * HD), jnp.bfloat16),
            pltpu.VMEM((groups * sec, 2 * HD), jnp.float32),
            pltpu.VMEM((groups * sec, HD), jnp.float32),
            pltpu.SemaphoreType.DMA,
        ],
        compiler_params=pltpu.CompilerParams(vmem_limit_bytes=48 * 2**20),
        cost_estimate=pl.CostEstimate(
            flops=8 * 10**9, bytes_accessed=6 * 10**6, transcendentals=16 * 10**6
        ),
        name="attend",
    )(coords, order, kept, starts, *q_pieces, *kv_pieces)


def project_kernel(coords, core, *refs):
    att_refs, weights = refs[:8], refs[8]
    own_out, other_out, att = refs[-3:]
    tok, wide = att_refs[0].shape

    @pl.when(pl.program_id(0) == 0)
    def _():
        for who in range(2):
            for j in range(4):
                head = wrap(coords[2] + SHIFTS[j])
                at = pl.multiple_of(head * wide, HD)
                att[pl.ds(who * tok, tok), pl.ds(at, wide)] = att_refs[4 * who + j][...]

    got = jnp.dot(att[...], weights[...], preferred_element_type=jnp.float32)
    got = got.astype(own_out.dtype)
    own_out[...] = got[:tok]
    other_out[...] = got[tok:]


def project(coords, core, own_att, other_att, weights, cols, half, whole):
    tok, wide = own_att[0].shape
    rows = RING * wide
    step = 2 * HD
    steps = cols // step
    piece = pl.BlockSpec((tok, wide), lambda i, *_: (0, 0))
    given = [] if whole is None else [whole]
    return pl.pallas_call(
        project_kernel,
        out_shape=[
            jax.ShapeDtypeStruct((tok, 4 * cols), jnp.bfloat16),
            jax.ShapeDtypeStruct((tok, cols), jnp.bfloat16),
        ],
        grid_spec=pltpu.PrefetchScalarGridSpec(
            num_scalar_prefetch=2,
            grid=(steps,),
            in_specs=[piece] * 8
            + [pl.BlockSpec((rows, step), lambda i, *_: (half, i))]
            + [pl.BlockSpec(memory_space=pl.ANY)] * len(given),
            out_specs=[
                pl.BlockSpec(
                    (tok, step), lambda i, where, core: (0, (half * 2 + core[0]) * steps + i)
                ),
                pl.BlockSpec((tok, step), lambda i, *_: (0, i)),
            ],
            scratch_shapes=[pltpu.VMEM((2 * tok, rows), jnp.bfloat16)],
        ),
        input_output_aliases={11: 0} if given else {},
        compiler_params=pltpu.CompilerParams(vmem_limit_bytes=48 * 2**20),
        cost_estimate=pl.CostEstimate(
            flops=3 * 10**9, bytes_accessed=9 * 10**6, transcendentals=0
        ),
        name="project",
    )(coords, core, *own_att, *other_att, weights, *given)


def merge_kernel(core, first, second, whole, out):
    del core, whole

    @pl.when(pl.program_id(0) == 0)
    def _():
        out[...] = first[...]

    @pl.when(pl.program_id(0) == 1)
    def _():
        out[...] = second[...]


def merge(core, theirs, whole):
    tok, cols = theirs[0].shape
    return pl.pallas_call(
        merge_kernel,
        out_shape=jax.ShapeDtypeStruct(whole.shape, whole.dtype),
        grid_spec=pltpu.PrefetchScalarGridSpec(
            num_scalar_prefetch=1,
            grid=(2,),
            in_specs=[pl.BlockSpec((tok, cols), lambda i, core: (0, 0))] * 2
            + [pl.BlockSpec(memory_space=pl.ANY)],
            out_specs=pl.BlockSpec((tok, cols), lambda i, core: (0, i * 2 + 1 - core[0])),
        ),
        input_output_aliases={3: 0},
        cost_estimate=pl.CostEstimate(flops=0, bytes_accessed=3 * 10**6, transcendentals=0),
        name="merge",
    )(core, *theirs, whole)


def per_device(query, keys, values, section_order, kept_sections, segment_ids, out_weight):
    tok = query.shape[1]
    sec = tok // 2
    nsec = section_order.shape[0]
    core = lax.axis_index("c")
    zl, x, y = lax.axis_index("zl"), lax.axis_index("x"), lax.axis_index("y")
    coords = jnp.stack([zl, x, y]).astype(jnp.int32)
    starts = jnp.stack([jnp.sum(segment_ids[0] < 1), jnp.sum(segment_ids[0] < 2)]).astype(jnp.int32)

    def head_slice(array, shift):
        wide = array.shape[2] // RING
        return lax.dynamic_slice_in_dim(array[0], wrap(y + shift) * wide, wide, 1)

    kv_pieces, q_pieces = [], []
    for shift in SHIFTS:
        kv = jnp.concatenate([head_slice(keys, -shift), head_slice(values, -shift)], axis=1)
        kv_pieces.append(kv if shift == 0 else shifted(kv, "y", -shift))
    for shift in SHIFTS:
        q = head_slice(query, -shift)
        q_pieces.append(q if shift == 0 else shifted(q, "y", -shift))
    near = jnp.stack(kv_pieces)
    far = shifted(near, "zl", 1, 2)
    kv_all = ring_gather(near)("x") + ring_gather(far)("x")

    cols = out_weight.shape[1]
    weights = lax.all_gather(out_weight, ("zh", "zl", "x", "y"), axis=0, tiled=True)

    attended = attention(
        coords, section_order, kept_sections[0], starts, q_pieces, kv_all, sec, nsec
    )
    by_shift = dict(zip(SHIFTS, attended))
    back = {0: by_shift[0]}
    for shift in SHIFTS[1:]:
        back[wrap_static(-shift)] = shifted(by_shift[shift], "y", shift)
    own_att = [back[s] for s in SHIFTS]
    other_att = [shifted(a, "c", 1, 2) for a in own_att]
    which = core[None].astype(jnp.int32)
    whole, theirs = None, []
    for half in range(2):
        whole, for_other = project(
            coords, which, own_att, other_att, weights, cols, half, whole
        )
        theirs.append(shifted(for_other, "c", 1, 2))
    return merge(which, theirs, whole)[None]


def wrap_static(shift):
    return 2 if shift in (2, -2) else shift


def solution(mesh):
    fine = Mesh(mesh.devices.reshape(2, 2, 2, 4, 4), ("zh", "c", "zl", "x", "y"))
    dp, ctx = ("zh", "c"), ("zl", "x", "y")
    return jax.shard_map(
        per_device,
        mesh=fine,
        in_specs=(
            P(dp, ctx, None),
            P(dp, ctx, None),
            P(dp, ctx, None),
            P(),
            P(dp, None),
            P(dp, None),
            P(ctx, dp),
        ),
        out_specs=P(dp, ctx, None),
        check_vma=False,
    )
```

```python
import functools
import math

import jax
import jax.numpy as jnp
from jax import lax
from jax.experimental import pallas as pl
from jax.experimental.pallas import tpu as pltpu
from jax.sharding import Mesh, PartitionSpec as P

HD = 128
RING = 4
SHIFTS = (0, -1, 1, 2)
BLOCK_KEYS = 2048
TAIL_STEP = 256
LOADS = 5
ROW_TILE = 16


def shifted(array, axis, step, size=RING):
    return lax.ppermute(array, axis, [(i, (i + step) % size) for i in range(size)])


def ring_gather(array):
    def on(axis):
        half = array.shape[0] // 2
        from_left = shifted(array, axis, 1)
        from_right = shifted(array, axis, -1)
        far_head = shifted(from_left[:half], axis, 1)
        far_tail = shifted(from_right[half:], axis, -1)
        return array, from_left, from_right, far_head, far_tail

    return on


def wrap(value):
    return lax.rem(value + RING, RING)


def attention_kernel(
    groups, sec, nsec, coords, order, kept, starts, *refs
):
    q_refs, kv_refs, out_refs = refs[:4], refs[4:14], refs[14:18]
    held, q_all, out_all, acc, peak, sem = refs[18:]
    zl, x, y = coords[0], coords[1], coords[2]
    rows = nsec * sec
    factor = math.log2(math.e) / math.sqrt(HD)

    def copies(act):
        for side in range(2):
            own_zl = zl if side == 0 else 1 - zl
            base = side * 5
            for x_rel in range(4):
                abs_x = wrap(x + SHIFTS[x_rel])
                for y_rel in range(4):
                    abs_y = wrap(y + SHIFTS[y_rel])
                    if x_rel < 3:
                        source = kv_refs[base + x_rel].at[y_rel]
                    else:
                        source = kv_refs[base + 3 + y_rel // 2].at[y_rel % 2]
                    for part in range(2):
                        section = ((own_zl * RING + abs_x) * RING + abs_y) * 2 + part
                        at = pl.multiple_of(order[section] * sec, ROW_TILE)
                        act(
                            source.at[pl.ds(part * sec, sec), :],
                            held.at[pl.ds(at, sec), pl.ds(0, 2 * HD)],
                        )

    copies(lambda a, b: pltpu.make_async_copy(a, b, sem).start())
    pad = held.shape[0] - rows
    held[pl.ds(rows, pad), pl.ds(0, 2 * HD)] = jnp.zeros((pad, 2 * HD), held.dtype)
    held[:, pl.ds(2 * HD, HD)] = jnp.ones((held.shape[0], HD), held.dtype)
    copies(lambda a, b: pltpu.make_async_copy(a, b, sem).wait())

    first, second = starts[0], starts[1]

    def segment_start(pos):
        return jnp.where(pos >= second, second, jnp.where(pos >= first, first, 0))

    for piece in range(4):
        q_all[pl.ds(piece * 2 * sec, 2 * sec), :] = q_refs[piece][...]

    def one_section(index, _):
        piece, part = index // 2, lax.rem(index, 2)
        shift = jnp.where(piece == 1, -1, jnp.where(piece == 0, 0, piece - 1))
        section = ((zl * RING + x) * RING + wrap(y + shift)) * 2 + part
        place = order[section]
        begin = place * sec
        own_rows = pl.ds(pl.multiple_of(index * sec, ROW_TILE), sec)

        @pl.when(kept[place] == 0)
        def _():
            out_all[own_rows, :] = jnp.zeros((sec, groups * HD), out_all.dtype)

        @pl.when(kept[place] != 0)
        def _():
            key_first = segment_start(begin) // ROW_TILE * ROW_TILE
            last_start = segment_start(begin + sec - 1)
            full = (begin + sec - key_first) // BLOCK_KEYS
            tail_first = key_first + full * BLOCK_KEYS
            tail_steps = (begin + sec - tail_first + TAIL_STEP - 1) // TAIL_STEP
            peak[...] = jnp.full(peak.shape, -1e30, jnp.float32)
            acc[...] = jnp.zeros(acc.shape, jnp.float32)

            def step(first, width, masked):
                at = pl.multiple_of(first, ROW_TILE)
                keys = held[pl.ds(at, width), pl.ds(0, HD)]
                values = held[pl.ds(at, width), pl.ds(HD, 2 * HD)]
                if masked:
                    row_pos = begin + lax.broadcasted_iota(jnp.int32, (sec, 1), 0)
                    row_start = segment_start(row_pos)
                    key_pos = at + lax.broadcasted_iota(jnp.int32, (1, width), 1)
                    seen = (key_pos <= row_pos) & (key_pos >= row_start)
                def score(g):
                    got = lax.dot_general(
                        q_all[own_rows, pl.ds(g * HD, HD)],
                        keys,
                        (((1,), (1,)), ((), ())),
                        preferred_element_type=jnp.float32,
                    )
                    return jnp.where(seen, got, -1e30) if masked else got

                def weigh(g, got):
                    rows_g = pl.ds(g * sec, sec)
                    before = peak[rows_g, :]
                    top = jnp.maximum(before, jnp.max(got, axis=1, keepdims=True))
                    peak[rows_g, :] = top
                    scaled = top * factor
                    weights = jnp.exp2(
                        got * factor - jnp.concatenate([scaled] * (width // HD), axis=1)
                    ).astype(jnp.bfloat16)
                    return weights, jnp.exp2(before * factor - scaled)

                def add(g, weights, rescale):
                    rows_g = pl.ds(g * sec, sec)
                    acc[rows_g, :] = acc[rows_g, :] * jnp.concatenate(
                        [rescale, rescale], axis=1
                    ) + jnp.dot(weights, values, preferred_element_type=jnp.float32)

                ahead = score(0)
                waiting = None
                for g in range(groups):
                    got, ahead = ahead, score(g + 1) if g + 1 < groups else None
                    if waiting is not None:
                        add(g - 1, *waiting)
                    waiting = weigh(g, got)
                add(groups - 1, *waiting)

            def full_block(block, _):
                first = key_first + block * BLOCK_KEYS
                masked = (first < last_start) | (first + BLOCK_KEYS > begin)
                pl.when(masked)(lambda: step(first, BLOCK_KEYS, True))
                pl.when(jnp.logical_not(masked))(lambda: step(first, BLOCK_KEYS, False))
                return 0

            lax.fori_loop(0, full, full_block, 0)
            for steps in range(1, BLOCK_KEYS // TAIL_STEP + 1):
                pl.when(tail_steps == steps)(
                    lambda steps=steps: step(tail_first, steps * TAIL_STEP, True)
                )
            for g in range(groups):
                rows_g = pl.ds(g * sec, sec)
                out_all[own_rows, pl.ds(g * HD, HD)] = (
                    acc[rows_g, pl.ds(0, HD)] / acc[rows_g, pl.ds(HD, HD)]
                ).astype(out_all.dtype)

        return 0

    lax.fori_loop(0, 8, one_section, 0)
    for piece in range(4):
        out_refs[piece][...] = out_all[pl.ds(piece * 2 * sec, 2 * sec), :]


def attention(coords, order, kept, starts, q_pieces, kv_pieces, sec, nsec):
    groups = q_pieces[0].shape[1] // HD
    rows = nsec * sec
    smem = pl.BlockSpec(memory_space=pltpu.SMEM)
    vmem = pl.BlockSpec(memory_space=pltpu.VMEM)
    return pl.pallas_call(
        functools.partial(attention_kernel, groups, sec, nsec),
        out_shape=[jax.ShapeDtypeStruct(q.shape, q.dtype) for q in q_pieces],
        in_specs=[smem] * 4 + [vmem] * 4 + [pl.BlockSpec(memory_space=pl.ANY)] * 10,
        out_specs=[vmem] * 4,
        scratch_shapes=[
            pltpu.VMEM((rows + TAIL_STEP, 3 * HD), jnp.bfloat16),
            pltpu.VMEM((8 * sec, groups * HD), jnp.bfloat16),
            pltpu.VMEM((8 * sec, groups * HD), jnp.bfloat16),
            pltpu.VMEM((groups * sec, 2 * HD), jnp.float32),
            pltpu.VMEM((groups * sec, HD), jnp.float32),
            pltpu.SemaphoreType.DMA,
        ],
        compiler_params=pltpu.CompilerParams(vmem_limit_bytes=48 * 2**20),
        cost_estimate=pl.CostEstimate(
            flops=8 * 10**9, bytes_accessed=6 * 10**6, transcendentals=16 * 10**6
        ),
        name="attend",
    )(coords, order, kept, starts, *q_pieces, *kv_pieces)


def project_kernel(coords, core, *refs):
    att_refs, weights = refs[:8], refs[8]
    whole, other_out, att, held, own, sems = refs[9:]
    tok, wide = att_refs[0].shape
    cols = weights.shape[1]
    rows = RING * wide
    piece = rows // LOADS

    def loads(half):
        for i in range(LOADS):
            at = pl.ds(half * rows + i * piece, piece)
            yield pltpu.make_async_copy(weights.at[at, :], held.at[at, :], sems.at[half])

    def store(half):
        at = pl.multiple_of((half * 2 + core[0]) * cols, HD)
        return pltpu.make_async_copy(own.at[half], whole.at[:, pl.ds(at, cols)], sems.at[2 + half])

    for half in range(2):
        for load in loads(half):
            load.start()
    for who in range(2):
        for j in range(4):
            head = wrap(coords[2] + SHIFTS[j])
            at = pl.multiple_of(head * wide, HD)
            att[pl.ds(who * tok, tok), pl.ds(at, wide)] = att_refs[4 * who + j][...]
    for half in range(2):
        for load in loads(half):
            load.wait()
        for first in range(0, cols, 2 * HD):
            got = jnp.dot(
                att[...],
                held[pl.ds(half * rows, rows), pl.ds(first, 2 * HD)],
                preferred_element_type=jnp.float32,
            ).astype(own.dtype)
            own[half, :, pl.ds(first, 2 * HD)] = got[:tok]
            other_out[half, :, pl.ds(first, 2 * HD)] = got[tok:]
        store(half).start()
    for half in range(2):
        store(half).wait()


def project(coords, core, own_att, other_att, weights):
    tok, wide = own_att[0].shape
    rows, cols = RING * wide, weights.shape[1]
    smem = pl.BlockSpec(memory_space=pltpu.SMEM)
    vmem = pl.BlockSpec(memory_space=pltpu.VMEM)
    anywhere = pl.BlockSpec(memory_space=pl.ANY)
    return pl.pallas_call(
        project_kernel,
        out_shape=[
            jax.ShapeDtypeStruct((tok, 4 * cols), jnp.bfloat16),
            jax.ShapeDtypeStruct((2, tok, cols), jnp.bfloat16),
        ],
        in_specs=[smem] * 2 + [vmem] * 8 + [anywhere],
        out_specs=[anywhere, vmem],
        scratch_shapes=[
            pltpu.VMEM((2 * tok, rows), jnp.bfloat16),
            pltpu.VMEM((2 * rows, cols), jnp.bfloat16),
            pltpu.VMEM((2, tok, cols), jnp.bfloat16),
            pltpu.SemaphoreType.DMA((4,)),
        ],
        compiler_params=pltpu.CompilerParams(vmem_limit_bytes=48 * 2**20),
        cost_estimate=pl.CostEstimate(
            flops=6 * 10**9, bytes_accessed=18 * 10**6, transcendentals=0
        ),
        name="project",
    )(coords, core, *own_att, *other_att, weights)


def merge_kernel(core, theirs, whole, out, sems):
    del whole
    cols = theirs.shape[2]

    def store(half):
        at = pl.multiple_of((half * 2 + 1 - core[0]) * cols, HD)
        return pltpu.make_async_copy(theirs.at[half], out.at[:, pl.ds(at, cols)], sems.at[half])

    for half in range(2):
        store(half).start()
    for half in range(2):
        store(half).wait()


def merge(core, theirs, whole):
    anywhere = pl.BlockSpec(memory_space=pl.ANY)
    return pl.pallas_call(
        merge_kernel,
        out_shape=jax.ShapeDtypeStruct(whole.shape, whole.dtype),
        in_specs=[
            pl.BlockSpec(memory_space=pltpu.SMEM),
            pl.BlockSpec(memory_space=pltpu.VMEM),
            anywhere,
        ],
        out_specs=anywhere,
        scratch_shapes=[pltpu.SemaphoreType.DMA((2,))],
        input_output_aliases={2: 0},
        cost_estimate=pl.CostEstimate(flops=0, bytes_accessed=3 * 10**6, transcendentals=0),
        name="merge",
    )(core, theirs, whole)


def per_device(query, keys, values, section_order, kept_sections, segment_ids, out_weight):
    tok = query.shape[1]
    sec = tok // 2
    nsec = section_order.shape[0]
    core = lax.axis_index("c")
    zl, x, y = lax.axis_index("zl"), lax.axis_index("x"), lax.axis_index("y")
    coords = jnp.stack([zl, x, y]).astype(jnp.int32)
    starts = jnp.stack([jnp.sum(segment_ids[0] < 1), jnp.sum(segment_ids[0] < 2)]).astype(jnp.int32)

    def head_slice(array, shift):
        wide = array.shape[2] // RING
        return lax.dynamic_slice_in_dim(array[0], wrap(y + shift) * wide, wide, 1)

    kv_pieces, q_pieces = [], []
    for shift in SHIFTS:
        kv = jnp.concatenate([head_slice(keys, -shift), head_slice(values, -shift)], axis=1)
        kv_pieces.append(kv if shift == 0 else shifted(kv, "y", -shift))
    for shift in SHIFTS:
        q = head_slice(query, -shift)
        q_pieces.append(q if shift == 0 else shifted(q, "y", -shift))
    near = jnp.stack(kv_pieces)
    far = shifted(near, "zl", 1, 2)
    kv_all = ring_gather(near)("x") + ring_gather(far)("x")

    weights = lax.all_gather(out_weight, ("zh", "zl", "x", "y"), axis=0, tiled=True)

    attended = attention(
        coords, section_order, kept_sections[0], starts, q_pieces, kv_all, sec, nsec
    )
    by_shift = dict(zip(SHIFTS, attended))
    back = {0: by_shift[0]}
    for shift in SHIFTS[1:]:
        back[wrap_static(-shift)] = shifted(by_shift[shift], "y", shift)
    own_att = [back[s] for s in SHIFTS]
    other_att = [shifted(a, "c", 1, 2) for a in own_att]
    which = core[None].astype(jnp.int32)
    whole, for_other = project(coords, which, own_att, other_att, weights)
    return merge(which, shifted(for_other, "c", 1, 2), whole)[None]


def wrap_static(shift):
    return 2 if shift in (2, -2) else shift


def solution(mesh):
    fine = Mesh(mesh.devices.reshape(2, 2, 2, 4, 4), ("zh", "c", "zl", "x", "y"))
    dp, ctx = ("zh", "c"), ("zl", "x", "y")
    return jax.shard_map(
        per_device,
        mesh=fine,
        in_specs=(
            P(dp, ctx, None),
            P(dp, ctx, None),
            P(dp, ctx, None),
            P(),
            P(dp, None),
            P(dp, None),
            P(ctx, dp),
        ),
        out_specs=P(dp, ctx, None),
        check_vma=False,
    )
```

```python
import functools
import math

import jax
import jax.numpy as jnp
from jax import lax
from jax.experimental import pallas as pl
from jax.experimental.pallas import tpu as pltpu
from jax.sharding import Mesh, PartitionSpec as P

HD = 128
RING = 4
SHIFTS = (0, -1, 1, 2)
BLOCK_KEYS = 2048
TAIL_STEP = 256
LOADS = 5
SLABS = 2
ROW_TILE = 16


def shifted(array, axis, step, size=RING):
    return lax.ppermute(array, axis, [(i, (i + step) % size) for i in range(size)])


def after(array, *others):
    return lax.optimization_barrier((array,) + others)[0]


def ring_gather(array, axis, *before_far):
    half = array.shape[0] // 2
    from_left = shifted(array, axis, 1)
    from_right = shifted(array, axis, -1)
    far_head = shifted(after(from_left[:half], *before_far), axis, 1)
    far_tail = shifted(after(from_right[half:], *before_far), axis, -1)
    return array, from_left, from_right, far_head, far_tail


def wrap(value):
    return lax.rem(value + RING, RING)


def attention_kernel(
    groups, sec, nsec, shifts, table, *refs
):
    count = len(shifts)
    q_refs, kv_refs, out_refs = refs[:count], refs[count : count + 9], refs[count + 9 : 2 * count + 9]
    held, q_all, out_all, acc, peak, sem = refs[2 * count + 9 :]
    base = 2 * nsec
    zl, x, y = table[base + 2], table[base + 3], table[base + 4]
    rows = nsec * sec
    factor = math.log2(math.e) / math.sqrt(HD)

    def copies(act):
        for side in range(2):
            own_zl = zl if side == 0 else 1 - zl
            for x_rel in range(4):
                abs_x = wrap(x + SHIFTS[x_rel])
                for y_rel in range(4):
                    abs_y = wrap(y + SHIFTS[y_rel])
                    if side == 1:
                        source = kv_refs[5 + x_rel].at[y_rel]
                    elif x_rel < 3:
                        source = kv_refs[x_rel].at[y_rel]
                    else:
                        source = kv_refs[3 + y_rel // 2].at[y_rel % 2]
                    for part in range(2):
                        section = ((own_zl * RING + abs_x) * RING + abs_y) * 2 + part
                        at = pl.multiple_of(table[section] * sec, ROW_TILE)
                        act(
                            source.at[pl.ds(part * sec, sec), :],
                            held.at[pl.ds(at, sec), pl.ds(0, 2 * HD)],
                        )

    copies(lambda a, b: pltpu.make_async_copy(a, b, sem).start())
    pad = held.shape[0] - rows
    held[pl.ds(rows, pad), pl.ds(0, 2 * HD)] = jnp.zeros((pad, 2 * HD), held.dtype)
    held[:, pl.ds(2 * HD, HD)] = jnp.ones((held.shape[0], HD), held.dtype)
    copies(lambda a, b: pltpu.make_async_copy(a, b, sem).wait())

    first, second = table[base], table[base + 1]

    def segment_start(pos):
        return jnp.where(pos >= second, second, jnp.where(pos >= first, first, 0))

    for piece in range(count):
        q_all[pl.ds(piece * 2 * sec, 2 * sec), :] = q_refs[piece][...]

    def one_section(index, _):
        piece, part = index // 2, lax.rem(index, 2)
        shift = shifts[0]
        for i in range(1, count):
            shift = jnp.where(piece == i, shifts[i], shift)
        section = ((zl * RING + x) * RING + wrap(y + shift)) * 2 + part
        place = table[section]
        begin = place * sec
        own_rows = pl.ds(pl.multiple_of(index * sec, ROW_TILE), sec)

        @pl.when(table[nsec + place] == 0)
        def _():
            out_all[own_rows, :] = jnp.zeros((sec, groups * HD), out_all.dtype)

        @pl.when(table[nsec + place] != 0)
        def _():
            key_first = segment_start(begin) // ROW_TILE * ROW_TILE
            last_start = segment_start(begin + sec - 1)
            full = (begin + sec - key_first) // BLOCK_KEYS
            tail_first = key_first + full * BLOCK_KEYS
            tail_steps = (begin + sec - tail_first + TAIL_STEP - 1) // TAIL_STEP
            peak[...] = jnp.full(peak.shape, -1e30, jnp.float32)
            acc[...] = jnp.zeros(acc.shape, jnp.float32)

            def step(first, width, masked):
                at = pl.multiple_of(first, ROW_TILE)
                keys = held[pl.ds(at, width), pl.ds(0, HD)]
                values = held[pl.ds(at, width), pl.ds(HD, 2 * HD)]
                if masked:
                    row_pos = begin + lax.broadcasted_iota(jnp.int32, (sec, 1), 0)
                    row_start = segment_start(row_pos)
                    key_pos = at + lax.broadcasted_iota(jnp.int32, (1, width), 1)
                    seen = (key_pos <= row_pos) & (key_pos >= row_start)
                def score(g):
                    got = lax.dot_general(
                        q_all[own_rows, pl.ds(g * HD, HD)],
                        keys,
                        (((1,), (1,)), ((), ())),
                        preferred_element_type=jnp.float32,
                    )
                    return jnp.where(seen, got, -1e30) if masked else got

                def weigh(g, got):
                    rows_g = pl.ds(g * sec, sec)
                    before = peak[rows_g, :]
                    top = jnp.maximum(before, jnp.max(got, axis=1, keepdims=True))
                    peak[rows_g, :] = top
                    scaled = top * factor
                    weights = jnp.exp2(
                        got * factor - jnp.concatenate([scaled] * (width // HD), axis=1)
                    ).astype(jnp.bfloat16)
                    return weights, jnp.exp2(before * factor - scaled)

                def add(g, weights, rescale):
                    rows_g = pl.ds(g * sec, sec)
                    acc[rows_g, :] = acc[rows_g, :] * jnp.concatenate(
                        [rescale, rescale], axis=1
                    ) + jnp.dot(weights, values, preferred_element_type=jnp.float32)

                ahead = score(0)
                waiting = None
                for g in range(groups):
                    got, ahead = ahead, score(g + 1) if g + 1 < groups else None
                    if waiting is not None:
                        add(g - 1, *waiting)
                    waiting = weigh(g, got)
                add(groups - 1, *waiting)

            def full_block(block, _):
                first = key_first + block * BLOCK_KEYS
                masked = (first < last_start) | (first + BLOCK_KEYS > begin)
                pl.when(masked)(lambda: step(first, BLOCK_KEYS, True))
                pl.when(jnp.logical_not(masked))(lambda: step(first, BLOCK_KEYS, False))
                return 0

            lax.fori_loop(0, full, full_block, 0)
            for steps in range(1, BLOCK_KEYS // TAIL_STEP + 1):
                pl.when(tail_steps == steps)(
                    lambda steps=steps: step(tail_first, steps * TAIL_STEP, True)
                )
            for g in range(groups):
                rows_g = pl.ds(g * sec, sec)
                out_all[own_rows, pl.ds(g * HD, HD)] = (
                    acc[rows_g, pl.ds(0, HD)] / acc[rows_g, pl.ds(HD, HD)]
                ).astype(out_all.dtype)

        return 0

    lax.fori_loop(0, 2 * count, one_section, 0)
    for piece in range(count):
        out_refs[piece][...] = out_all[pl.ds(piece * 2 * sec, 2 * sec), :]


def attention(table, shifts, q_pieces, kv_pieces, sec, nsec):
    groups = q_pieces[0].shape[1] // HD
    rows = nsec * sec
    count = len(shifts)
    smem = pl.BlockSpec(memory_space=pltpu.SMEM)
    vmem = pl.BlockSpec(memory_space=pltpu.VMEM)
    return pl.pallas_call(
        functools.partial(attention_kernel, groups, sec, nsec, shifts),
        out_shape=[jax.ShapeDtypeStruct(q.shape, q.dtype) for q in q_pieces],
        in_specs=[smem] + [vmem] * count + [pl.BlockSpec(memory_space=pl.ANY)] * 9,
        out_specs=[vmem] * count,
        scratch_shapes=[
            pltpu.VMEM((rows + TAIL_STEP, 3 * HD), jnp.bfloat16),
            pltpu.VMEM((2 * count * sec, groups * HD), jnp.bfloat16),
            pltpu.VMEM((2 * count * sec, groups * HD), jnp.bfloat16),
            pltpu.VMEM((groups * sec, 2 * HD), jnp.float32),
            pltpu.VMEM((groups * sec, HD), jnp.float32),
            pltpu.SemaphoreType.DMA,
        ],
        compiler_params=pltpu.CompilerParams(vmem_limit_bytes=48 * 2**20),
        cost_estimate=pl.CostEstimate(
            flops=count * 2 * 10**9,
            bytes_accessed=6 * 10**6,
            transcendentals=count * 4 * 10**6,
        ),
        name="attend",
    )(table, *q_pieces, *kv_pieces)


def project_kernel(base, slabs, table, *refs):
    att_refs, weights, ring_refs = refs[:8], refs[8], refs[9:14]
    whole, other_out, att, held, ring_held, own, sems = refs[14:]
    tok, wide = att_refs[0].shape
    cols = weights.shape[1]
    slab = ring_refs[0].shape[3]
    depth = ring_refs[0].shape[2] // slabs
    all_cols = cols + slabs * slab
    rows = RING * wide
    piece = rows // LOADS
    x, y, z, core = (table[base + i] for i in (3, 4, 5, 6))

    def ring_loads(act):
        def for_y(i, _):
            shift = jnp.where(i == 0, 0, jnp.where(i == 1, -1, jnp.where(i == 2, 1, 2)))
            abs_y = wrap(y + shift)
            for j in range(4):
                abs_x = wrap(x + SHIFTS[j])
                for k in range(4):
                    abs_z = wrap(z + SHIFTS[k])
                    row = ((lax.rem(abs_z, 2) * RING + abs_x) * RING + abs_y) * depth
                    row = pl.multiple_of(row, ROW_TILE)
                    source = ring_refs[k].at[j, i] if k < 3 else ring_refs[3 + j // 2].at[j % 2, i]
                    for m in range(slabs):
                        col = pl.multiple_of((abs_z // 2 * slabs + m) * slab, HD)
                        act(
                            pltpu.make_async_copy(
                                source.at[pl.ds(m * depth, depth), :],
                                ring_held.at[pl.ds(row, depth), pl.ds(col, slab)],
                                sems.at[4],
                            )
                        )
            return 0

        lax.fori_loop(0, 4, for_y, 0)

    def loads(half):
        for i in range(LOADS):
            at = pl.ds(half * rows + i * piece, piece)
            yield pltpu.make_async_copy(weights.at[at, :], held.at[at, :], sems.at[half])

    def store(half):
        at = pl.multiple_of((half * 2 + core) * all_cols, HD)
        return pltpu.make_async_copy(
            own.at[half], whole.at[:, pl.ds(at, all_cols)], sems.at[2 + half]
        )

    def multiply(half, block, at):
        got = jnp.dot(att[...], block, preferred_element_type=jnp.float32).astype(own.dtype)
        own[half, :, at] = got[:tok]
        other_out[half, :, at] = got[tok:]

    ring_loads(lambda copy: copy.start())
    for half in range(2):
        for load in loads(half):
            load.start()
    for who in range(2):
        for j in range(4):
            head = wrap(y + SHIFTS[j])
            at = pl.multiple_of(head * wide, HD)
            att[pl.ds(who * tok, tok), pl.ds(at, wide)] = att_refs[4 * who + j][...]
    ring_loads(lambda copy: copy.wait())
    for half in range(2):
        for m in range(slabs):
            multiply(
                half,
                ring_held[:, pl.ds((half * slabs + m) * slab, slab)],
                pl.ds(cols + m * slab, slab),
            )
    for half in range(2):
        for load in loads(half):
            load.wait()
        for first in range(0, cols, 2 * HD):
            multiply(
                half,
                held[pl.ds(half * rows, rows), pl.ds(first, 2 * HD)],
                pl.ds(first, 2 * HD),
            )
        store(half).start()
    for half in range(2):
        store(half).wait()


def project(table, base, own_att, other_att, weights, ring_pieces, slabs):
    tok, wide = own_att[0].shape
    rows, cols = RING * wide, weights.shape[1]
    slab = ring_pieces[0].shape[3]
    all_cols = cols + slabs * slab
    smem = pl.BlockSpec(memory_space=pltpu.SMEM)
    vmem = pl.BlockSpec(memory_space=pltpu.VMEM)
    anywhere = pl.BlockSpec(memory_space=pl.ANY)
    return pl.pallas_call(
        functools.partial(project_kernel, base, slabs),
        out_shape=[
            jax.ShapeDtypeStruct((tok, 4 * all_cols), jnp.bfloat16),
            jax.ShapeDtypeStruct((2, tok, all_cols), jnp.bfloat16),
        ],
        in_specs=[smem] + [vmem] * 8 + [anywhere] * 6,
        out_specs=[anywhere, vmem],
        scratch_shapes=[
            pltpu.VMEM((2 * tok, rows), jnp.bfloat16),
            pltpu.VMEM((2 * rows, cols), jnp.bfloat16),
            pltpu.VMEM((rows, 2 * slabs * slab), jnp.bfloat16),
            pltpu.VMEM((2, tok, all_cols), jnp.bfloat16),
            pltpu.SemaphoreType.DMA((5,)),
        ],
        compiler_params=pltpu.CompilerParams(vmem_limit_bytes=48 * 2**20),
        cost_estimate=pl.CostEstimate(
            flops=6 * 10**9, bytes_accessed=18 * 10**6, transcendentals=0
        ),
        name="project",
    )(table, *own_att, *other_att, weights, *ring_pieces)


def merge_kernel(base, table, theirs, whole, out, sems):
    del whole
    cols = theirs.shape[2]

    def store(half):
        at = pl.multiple_of((half * 2 + 1 - table[base + 6]) * cols, HD)
        return pltpu.make_async_copy(theirs.at[half], out.at[:, pl.ds(at, cols)], sems.at[half])

    for half in range(2):
        store(half).start()
    for half in range(2):
        store(half).wait()


def merge(table, base, theirs, whole):
    anywhere = pl.BlockSpec(memory_space=pl.ANY)
    return pl.pallas_call(
        functools.partial(merge_kernel, base),
        out_shape=jax.ShapeDtypeStruct(whole.shape, whole.dtype),
        in_specs=[
            pl.BlockSpec(memory_space=pltpu.SMEM),
            pl.BlockSpec(memory_space=pltpu.VMEM),
            anywhere,
        ],
        out_specs=anywhere,
        scratch_shapes=[pltpu.SemaphoreType.DMA((2,))],
        input_output_aliases={2: 0},
        cost_estimate=pl.CostEstimate(flops=0, bytes_accessed=3 * 10**6, transcendentals=0),
        name="merge",
    )(table, theirs, whole)


def per_device(query, keys, values, section_order, kept_sections, segment_ids, out_weight):
    tok = query.shape[1]
    sec = tok // 2
    nsec = section_order.shape[0]
    zh, core = lax.axis_index("zh"), lax.axis_index("c")
    zl, x, y = lax.axis_index("zl"), lax.axis_index("x"), lax.axis_index("y")
    first, second = jnp.sum(segment_ids[0] < 1), jnp.sum(segment_ids[0] < 2)
    scalars = jnp.stack([first, second, zl, x, y, zh * 2 + zl, core]).astype(jnp.int32)
    table = jnp.concatenate([section_order, kept_sections[0], scalars])

    def head_slice(array, shift):
        wide = array.shape[2] // RING
        return lax.dynamic_slice_in_dim(array[0], wrap(y + shift) * wide, wide, 1)

    cols = out_weight.shape[1]
    slab = 2 * HD
    rest = cols - SLABS * slab
    weights = lax.all_gather(out_weight[:, :rest], ("zh", "zl", "x", "y"), axis=0, tiled=True)
    slices = [out_weight[:, rest + m * slab : rest + (m + 1) * slab] for m in range(SLABS)]

    carried, q_pieces = [], []
    for shift in SHIFTS:
        kv = jnp.concatenate([head_slice(keys, -shift), head_slice(values, -shift)], axis=1)
        load = jnp.concatenate([kv] + slices, axis=0)
        carried.append(load if shift == 0 else shifted(load, "y", -shift))
    for shift in SHIFTS:
        q = head_slice(query, -shift)
        q_pieces.append(q if shift == 0 else shifted(q, "y", -shift))
    far = shifted(jnp.stack([c[:tok] for c in carried]), "zl", 1, 2)
    near = ring_gather(jnp.stack(carried), "x", far)
    opposite = jnp.concatenate([near[3], near[4]], axis=0)
    far_all = (
        far,
        shifted(far, "x", 1),
        shifted(far, "x", -1),
        shifted(opposite[:, :tok], "zl", 1, 2),
    )
    kv_all = near + far_all
    attended = attention(table, SHIFTS[1:], q_pieces[1:], kv_all, sec, nsec)
    plane = jnp.stack([part[:, tok:] for part in near[:3] + (opposite,)])
    plane = after(plane, far_all[1], far_all[2], *q_pieces[1:])
    own_query = after(q_pieces[0], attended[0])
    attended = attention(table, SHIFTS[:1], [own_query], kv_all, sec, nsec) + attended
    by_shift = dict(zip(SHIFTS, attended))
    back = {0: by_shift[0]}
    for shift in SHIFTS[1:]:
        back[wrap_static(-shift)] = shifted(by_shift[shift], "y", shift)
    ring_pieces = ring_gather(plane, ("zh", "zl"), back[1])
    own_att = [back[s] for s in SHIFTS]
    other_att = [shifted(a, "c", 1, 2) for a in own_att]
    base = 2 * nsec
    whole, for_other = project(table, base, own_att, other_att, weights, ring_pieces, SLABS)
    return merge(table, base, shifted(for_other, "c", 1, 2), whole)[None]


def wrap_static(shift):
    return 2 if shift in (2, -2) else shift


def solution(mesh):
    fine = Mesh(mesh.devices.reshape(2, 2, 2, 4, 4), ("zh", "c", "zl", "x", "y"))
    dp, ctx = ("zh", "c"), ("zl", "x", "y")
    return jax.shard_map(
        per_device,
        mesh=fine,
        in_specs=(
            P(dp, ctx, None),
            P(dp, ctx, None),
            P(dp, ctx, None),
            P(),
            P(dp, None),
            P(dp, None),
            P(ctx, dp),
        ),
        out_specs=P(dp, ctx, None),
        check_vma=False,
    )
```

```python
import functools
import math

import jax
import jax.numpy as jnp
from jax import lax
from jax.experimental import pallas as pl
from jax.experimental.pallas import tpu as pltpu
from jax.sharding import Mesh, PartitionSpec as P

HD = 128
RING = 4
SHIFTS = (0, -1, 1, 2)
BLOCK_KEYS = 2048
TAIL_STEP = 256
LOADS = 5
SLABS = 1
ROW_TILE = 16


def shifted(array, axis, step, size=RING):
    return lax.ppermute(array, axis, [(i, (i + step) % size) for i in range(size)])


def after(array, *others):
    return lax.optimization_barrier((array,) + others)[0]


def ring_gather(array, axis, *before_far):
    half = array.shape[0] // 2
    from_left = shifted(array, axis, 1)
    from_right = shifted(array, axis, -1)
    far_head = shifted(after(from_left[:half], *before_far), axis, 1)
    far_tail = shifted(after(from_right[half:], *before_far), axis, -1)
    return array, from_left, from_right, far_head, far_tail


def wrap(value):
    return lax.rem(value + RING, RING)


def attention_kernel(
    groups, sec, nsec, shifts, table, *refs
):
    count = len(shifts)
    q_refs, kv_refs, out_refs = refs[:count], refs[count : count + 9], refs[count + 9 : 2 * count + 9]
    held, q_all, out_all, acc, peak, sem = refs[2 * count + 9 :]
    base = 2 * nsec
    zl, x, y = table[base + 2], table[base + 3], table[base + 4]
    rows = nsec * sec
    factor = math.log2(math.e) / math.sqrt(HD)

    def copies(act):
        for side in range(2):
            own_zl = zl if side == 0 else 1 - zl
            for x_rel in range(4):
                abs_x = wrap(x + SHIFTS[x_rel])
                for y_rel in range(4):
                    abs_y = wrap(y + SHIFTS[y_rel])
                    if side == 1:
                        source = kv_refs[5 + x_rel].at[y_rel]
                    elif x_rel < 3:
                        source = kv_refs[x_rel].at[y_rel]
                    else:
                        source = kv_refs[3 + y_rel // 2].at[y_rel % 2]
                    for part in range(2):
                        section = ((own_zl * RING + abs_x) * RING + abs_y) * 2 + part
                        at = pl.multiple_of(table[section] * sec, ROW_TILE)
                        act(
                            source.at[pl.ds(part * sec, sec), :],
                            held.at[pl.ds(at, sec), pl.ds(0, 2 * HD)],
                        )

    copies(lambda a, b: pltpu.make_async_copy(a, b, sem).start())
    pad = held.shape[0] - rows
    held[pl.ds(rows, pad), pl.ds(0, 2 * HD)] = jnp.zeros((pad, 2 * HD), held.dtype)
    held[:, pl.ds(2 * HD, HD)] = jnp.ones((held.shape[0], HD), held.dtype)
    copies(lambda a, b: pltpu.make_async_copy(a, b, sem).wait())

    first, second = table[base], table[base + 1]

    def segment_start(pos):
        return jnp.where(pos >= second, second, jnp.where(pos >= first, first, 0))

    for piece in range(count):
        q_all[pl.ds(piece * 2 * sec, 2 * sec), :] = q_refs[piece][...]

    def one_section(index, _):
        piece, part = index // 2, lax.rem(index, 2)
        shift = shifts[0]
        for i in range(1, count):
            shift = jnp.where(piece == i, shifts[i], shift)
        section = ((zl * RING + x) * RING + wrap(y + shift)) * 2 + part
        place = table[section]
        begin = place * sec
        own_rows = pl.ds(pl.multiple_of(index * sec, ROW_TILE), sec)

        @pl.when(table[nsec + place] == 0)
        def _():
            out_all[own_rows, :] = jnp.zeros((sec, groups * HD), out_all.dtype)

        @pl.when(table[nsec + place] != 0)
        def _():
            key_first = segment_start(begin) // ROW_TILE * ROW_TILE
            last_start = segment_start(begin + sec - 1)
            full = (begin + sec - key_first) // BLOCK_KEYS
            tail_first = key_first + full * BLOCK_KEYS
            tail_steps = (begin + sec - tail_first + TAIL_STEP - 1) // TAIL_STEP
            peak[...] = jnp.full(peak.shape, -1e30, jnp.float32)
            acc[...] = jnp.zeros(acc.shape, jnp.float32)

            def step(first, width, masked):
                at = pl.multiple_of(first, ROW_TILE)
                keys = held[pl.ds(at, width), pl.ds(0, HD)]
                values = held[pl.ds(at, width), pl.ds(HD, 2 * HD)]
                if masked:
                    row_pos = begin + lax.broadcasted_iota(jnp.int32, (sec, 1), 0)
                    row_start = segment_start(row_pos)
                    key_pos = at + lax.broadcasted_iota(jnp.int32, (1, width), 1)
                    seen = (key_pos <= row_pos) & (key_pos >= row_start)
                def score(g):
                    got = lax.dot_general(
                        q_all[own_rows, pl.ds(g * HD, HD)],
                        keys,
                        (((1,), (1,)), ((), ())),
                        preferred_element_type=jnp.float32,
                    )
                    return jnp.where(seen, got, -1e30) if masked else got

                def weigh(g, got):
                    rows_g = pl.ds(g * sec, sec)
                    before = peak[rows_g, :]
                    top = jnp.maximum(before, jnp.max(got, axis=1, keepdims=True))
                    peak[rows_g, :] = top
                    scaled = top * factor
                    weights = jnp.exp2(
                        got * factor - jnp.concatenate([scaled] * (width // HD), axis=1)
                    ).astype(jnp.bfloat16)
                    return weights, jnp.exp2(before * factor - scaled)

                def add(g, weights, rescale):
                    rows_g = pl.ds(g * sec, sec)
                    acc[rows_g, :] = acc[rows_g, :] * jnp.concatenate(
                        [rescale, rescale], axis=1
                    ) + jnp.dot(weights, values, preferred_element_type=jnp.float32)

                ahead = score(0)
                waiting = None
                for g in range(groups):
                    got, ahead = ahead, score(g + 1) if g + 1 < groups else None
                    if waiting is not None:
                        add(g - 1, *waiting)
                    waiting = weigh(g, got)
                add(groups - 1, *waiting)

            def full_block(block, _):
                first = key_first + block * BLOCK_KEYS
                masked = (first < last_start) | (first + BLOCK_KEYS > begin)
                pl.when(masked)(lambda: step(first, BLOCK_KEYS, True))
                pl.when(jnp.logical_not(masked))(lambda: step(first, BLOCK_KEYS, False))
                return 0

            lax.fori_loop(0, full, full_block, 0)
            for steps in range(1, BLOCK_KEYS // TAIL_STEP + 1):
                pl.when(tail_steps == steps)(
                    lambda steps=steps: step(tail_first, steps * TAIL_STEP, True)
                )
            for g in range(groups):
                rows_g = pl.ds(g * sec, sec)
                out_all[own_rows, pl.ds(g * HD, HD)] = (
                    acc[rows_g, pl.ds(0, HD)] / acc[rows_g, pl.ds(HD, HD)]
                ).astype(out_all.dtype)

        return 0

    lax.fori_loop(0, 2 * count, one_section, 0)
    for piece in range(count):
        out_refs[piece][...] = out_all[pl.ds(piece * 2 * sec, 2 * sec), :]


def attention(table, shifts, q_pieces, kv_pieces, sec, nsec):
    groups = q_pieces[0].shape[1] // HD
    rows = nsec * sec
    count = len(shifts)
    smem = pl.BlockSpec(memory_space=pltpu.SMEM)
    vmem = pl.BlockSpec(memory_space=pltpu.VMEM)
    return pl.pallas_call(
        functools.partial(attention_kernel, groups, sec, nsec, shifts),
        out_shape=[jax.ShapeDtypeStruct(q.shape, q.dtype) for q in q_pieces],
        in_specs=[smem] + [vmem] * count + [pl.BlockSpec(memory_space=pl.ANY)] * 9,
        out_specs=[vmem] * count,
        scratch_shapes=[
            pltpu.VMEM((rows + TAIL_STEP, 3 * HD), jnp.bfloat16),
            pltpu.VMEM((2 * count * sec, groups * HD), jnp.bfloat16),
            pltpu.VMEM((2 * count * sec, groups * HD), jnp.bfloat16),
            pltpu.VMEM((groups * sec, 2 * HD), jnp.float32),
            pltpu.VMEM((groups * sec, HD), jnp.float32),
            pltpu.SemaphoreType.DMA,
        ],
        compiler_params=pltpu.CompilerParams(vmem_limit_bytes=24 * 2**20),
        cost_estimate=pl.CostEstimate(
            flops=count * 2 * 10**9,
            bytes_accessed=6 * 10**6,
            transcendentals=count * 4 * 10**6,
        ),
        name="attend",
    )(table, *q_pieces, *kv_pieces)


def project_kernel(base, slabs, table, *refs):
    att_refs, weights, ring_refs = refs[:8], refs[8], refs[9:14]
    whole, other_out, att, held, ring_held, own, sems = refs[14:]
    tok, wide = att_refs[0].shape
    cols = weights.shape[1]
    slab = ring_refs[0].shape[3]
    depth = ring_refs[0].shape[2] // slabs
    all_cols = cols + slabs * slab
    rows = RING * wide
    piece = rows // LOADS
    x, y, z, core = (table[base + i] for i in (3, 4, 5, 6))

    def ring_loads(act):
        def for_y(i, _):
            shift = jnp.where(i == 0, 0, jnp.where(i == 1, -1, jnp.where(i == 2, 1, 2)))
            abs_y = wrap(y + shift)
            for j in range(4):
                abs_x = wrap(x + SHIFTS[j])
                for k in range(4):
                    abs_z = wrap(z + SHIFTS[k])
                    row = ((lax.rem(abs_z, 2) * RING + abs_x) * RING + abs_y) * depth
                    row = pl.multiple_of(row, ROW_TILE)
                    source = ring_refs[k].at[j, i] if k < 3 else ring_refs[3 + j // 2].at[j % 2, i]
                    for m in range(slabs):
                        col = pl.multiple_of((abs_z // 2 * slabs + m) * slab, HD)
                        act(
                            pltpu.make_async_copy(
                                source.at[pl.ds(m * depth, depth), :],
                                ring_held.at[pl.ds(row, depth), pl.ds(col, slab)],
                                sems.at[4],
                            )
                        )
            return 0

        lax.fori_loop(0, 4, for_y, 0)

    def loads(half):
        for i in range(LOADS):
            at = pl.ds(half * rows + i * piece, piece)
            yield pltpu.make_async_copy(weights.at[at, :], held.at[at, :], sems.at[half])

    def store(half):
        at = pl.multiple_of((half * 2 + core) * all_cols, HD)
        return pltpu.make_async_copy(
            own.at[half], whole.at[:, pl.ds(at, all_cols)], sems.at[2 + half]
        )

    def multiply(half, block, at):
        got = jnp.dot(att[...], block, preferred_element_type=jnp.float32).astype(own.dtype)
        own[half, :, at] = got[:tok]
        other_out[half, :, at] = got[tok:]

    ring_loads(lambda copy: copy.start())
    for half in range(2):
        for load in loads(half):
            load.start()
    for who in range(2):
        for j in range(4):
            head = wrap(y + SHIFTS[j])
            at = pl.multiple_of(head * wide, HD)
            att[pl.ds(who * tok, tok), pl.ds(at, wide)] = att_refs[4 * who + j][...]
    ring_loads(lambda copy: copy.wait())
    for half in range(2):
        for m in range(slabs):
            multiply(
                half,
                ring_held[:, pl.ds((half * slabs + m) * slab, slab)],
                pl.ds(cols + m * slab, slab),
            )
    for half in range(2):
        for load in loads(half):
            load.wait()
        for first in range(0, cols, 2 * HD):
            multiply(
                half,
                held[pl.ds(half * rows, rows), pl.ds(first, 2 * HD)],
                pl.ds(first, 2 * HD),
            )
        store(half).start()
    for half in range(2):
        store(half).wait()


def project(table, base, own_att, other_att, weights, ring_pieces, slabs):
    tok, wide = own_att[0].shape
    rows, cols = RING * wide, weights.shape[1]
    slab = ring_pieces[0].shape[3]
    all_cols = cols + slabs * slab
    smem = pl.BlockSpec(memory_space=pltpu.SMEM)
    vmem = pl.BlockSpec(memory_space=pltpu.VMEM)
    anywhere = pl.BlockSpec(memory_space=pl.ANY)
    return pl.pallas_call(
        functools.partial(project_kernel, base, slabs),
        out_shape=[
            jax.ShapeDtypeStruct((tok, 4 * all_cols), jnp.bfloat16),
            jax.ShapeDtypeStruct((2, tok, all_cols), jnp.bfloat16),
        ],
        in_specs=[smem] + [vmem] * 8 + [anywhere] * 6,
        out_specs=[anywhere, vmem],
        scratch_shapes=[
            pltpu.VMEM((2 * tok, rows), jnp.bfloat16),
            pltpu.VMEM((2 * rows, cols), jnp.bfloat16),
            pltpu.VMEM((rows, 2 * slabs * slab), jnp.bfloat16),
            pltpu.VMEM((2, tok, all_cols), jnp.bfloat16),
            pltpu.SemaphoreType.DMA((5,)),
        ],
        compiler_params=pltpu.CompilerParams(vmem_limit_bytes=32 * 2**20),
        cost_estimate=pl.CostEstimate(
            flops=6 * 10**9, bytes_accessed=18 * 10**6, transcendentals=0
        ),
        name="project",
    )(table, *own_att, *other_att, weights, *ring_pieces)


def merge_kernel(base, table, theirs, whole, out, sems):
    del whole
    cols = theirs.shape[2]

    def store(half):
        at = pl.multiple_of((half * 2 + 1 - table[base + 6]) * cols, HD)
        return pltpu.make_async_copy(theirs.at[half], out.at[:, pl.ds(at, cols)], sems.at[half])

    for half in range(2):
        store(half).start()
    for half in range(2):
        store(half).wait()


def merge(table, base, theirs, whole):
    anywhere = pl.BlockSpec(memory_space=pl.ANY)
    return pl.pallas_call(
        functools.partial(merge_kernel, base),
        out_shape=jax.ShapeDtypeStruct(whole.shape, whole.dtype),
        in_specs=[
            pl.BlockSpec(memory_space=pltpu.SMEM),
            pl.BlockSpec(memory_space=pltpu.VMEM),
            anywhere,
        ],
        out_specs=anywhere,
        scratch_shapes=[pltpu.SemaphoreType.DMA((2,))],
        input_output_aliases={2: 0},
        cost_estimate=pl.CostEstimate(flops=0, bytes_accessed=3 * 10**6, transcendentals=0),
        name="merge",
    )(table, theirs, whole)


def per_device(query, keys, values, section_order, kept_sections, segment_ids, out_weight):
    tok = query.shape[1]
    sec = tok // 2
    nsec = section_order.shape[0]
    zh, core = lax.axis_index("zh"), lax.axis_index("c")
    zl, x, y = lax.axis_index("zl"), lax.axis_index("x"), lax.axis_index("y")
    first, second = jnp.sum(segment_ids[0] < 1), jnp.sum(segment_ids[0] < 2)
    scalars = jnp.stack([first, second, zl, x, y, zh * 2 + zl, core]).astype(jnp.int32)
    table = jnp.concatenate([section_order, kept_sections[0], scalars])

    def head_slice(array, shift):
        wide = array.shape[2] // RING
        return lax.dynamic_slice_in_dim(array[0], wrap(y + shift) * wide, wide, 1)

    cols = out_weight.shape[1]
    slab = 2 * HD
    rest = cols - SLABS * slab
    weights = lax.all_gather(out_weight[:, :rest], ("zh", "zl", "x", "y"), axis=0, tiled=True)
    slices = [out_weight[:, rest + m * slab : rest + (m + 1) * slab] for m in range(SLABS)]

    carried, q_pieces = [], []
    for shift in SHIFTS:
        kv = jnp.concatenate([head_slice(keys, -shift), head_slice(values, -shift)], axis=1)
        load = jnp.concatenate([kv] + slices, axis=0)
        carried.append(load if shift == 0 else shifted(load, "y", -shift))
    far = shifted(jnp.stack([c[:tok] for c in carried]), "zl", 1, 2)
    near = ring_gather(jnp.stack(carried), "x", far)
    opposite = jnp.concatenate([near[3], near[4]], axis=0)
    far_all = (
        far,
        shifted(far, "x", 1),
        shifted(far, "x", -1),
        shifted(opposite[:, :tok], "zl", 1, 2),
    )
    kv_all = near + far_all
    for shift in SHIFTS:
        q = head_slice(after(query, far, near[1], near[2]), -shift)
        q_pieces.append(q if shift == 0 else shifted(q, "y", -shift))
    attended = attention(table, SHIFTS[1:], q_pieces[1:], kv_all, sec, nsec)
    plane = jnp.stack([part[:, tok:] for part in near[:3] + (opposite,)])
    plane = after(plane, *far_all, *q_pieces[1:])
    own_query = after(q_pieces[0], attended[0])
    attended = attention(table, SHIFTS[:1], [own_query], kv_all, sec, nsec) + attended
    by_shift = dict(zip(SHIFTS, attended))
    back = {0: by_shift[0]}
    for shift in SHIFTS[1:]:
        back[wrap_static(-shift)] = shifted(by_shift[shift], "y", shift)
    ring_pieces = ring_gather(plane, ("zh", "zl"), back[1])
    own_att = [back[s] for s in SHIFTS]
    other_att = [shifted(a, "c", 1, 2) for a in own_att]
    base = 2 * nsec
    whole, for_other = project(table, base, own_att, other_att, weights, ring_pieces, SLABS)
    return merge(table, base, shifted(for_other, "c", 1, 2), whole)[None]


def wrap_static(shift):
    return 2 if shift in (2, -2) else shift


def solution(mesh):
    fine = Mesh(mesh.devices.reshape(2, 2, 2, 4, 4), ("zh", "c", "zl", "x", "y"))
    dp, ctx = ("zh", "c"), ("zl", "x", "y")
    return jax.shard_map(
        per_device,
        mesh=fine,
        in_specs=(
            P(dp, ctx, None),
            P(dp, ctx, None),
            P(dp, ctx, None),
            P(),
            P(dp, None),
            P(dp, None),
            P(ctx, dp),
        ),
        out_specs=P(dp, ctx, None),
        check_vma=False,
    )
```

```python
import functools
import math

import jax
import jax.numpy as jnp
from jax import lax
from jax.experimental import pallas as pl
from jax.experimental.pallas import tpu as pltpu
from jax.sharding import Mesh, PartitionSpec as P

HD = 128
RING = 4
SHIFTS = (0, -1, 1, 2)
BLOCK_KEYS = 2048
TAIL_STEP = 256
ROW_TILE = 16


def shifted(array, axis, step, size=RING):
    return lax.ppermute(array, axis, [(i, (i + step) % size) for i in range(size)])


def ring_gather(array, axis):
    half = array.shape[0] // 2
    from_left = shifted(array, axis, 1)
    from_right = shifted(array, axis, -1)
    far_head = shifted(from_left[:half], axis, 1)
    far_tail = shifted(from_right[half:], axis, -1)
    return array, from_left, from_right, far_head, far_tail


def wrap(value):
    return lax.rem(value + RING, RING)


def attention_kernel(
    groups, sec, nsec, shifts, table, *refs
):
    count = len(shifts)
    q_refs, kv_refs, out_refs = refs[:count], refs[count : count + 9], refs[count + 9 : 2 * count + 9]
    held, q_all, out_all, acc, peak, sem = refs[2 * count + 9 :]
    base = 2 * nsec
    zl, x, y = table[base + 2], table[base + 3], table[base + 4]
    rows = nsec * sec
    factor = math.log2(math.e) / math.sqrt(HD)

    def copies(act):
        for side in range(2):
            own_zl = zl if side == 0 else 1 - zl
            for x_rel in range(4):
                abs_x = wrap(x + SHIFTS[x_rel])
                for y_rel in range(4):
                    abs_y = wrap(y + SHIFTS[y_rel])
                    if side == 1:
                        source = kv_refs[5 + x_rel].at[y_rel]
                    elif x_rel < 3:
                        source = kv_refs[x_rel].at[y_rel]
                    else:
                        source = kv_refs[3 + y_rel // 2].at[y_rel % 2]
                    for part in range(2):
                        section = ((own_zl * RING + abs_x) * RING + abs_y) * 2 + part
                        at = pl.multiple_of(table[section] * sec, ROW_TILE)
                        act(
                            source.at[pl.ds(part * sec, sec), :],
                            held.at[pl.ds(at, sec), pl.ds(0, 2 * HD)],
                        )

    copies(lambda a, b: pltpu.make_async_copy(a, b, sem).start())
    pad = held.shape[0] - rows
    held[pl.ds(rows, pad), pl.ds(0, 2 * HD)] = jnp.zeros((pad, 2 * HD), held.dtype)
    held[:, pl.ds(2 * HD, HD)] = jnp.ones((held.shape[0], HD), held.dtype)
    copies(lambda a, b: pltpu.make_async_copy(a, b, sem).wait())

    first, second = table[base], table[base + 1]

    def segment_start(pos):
        return jnp.where(pos >= second, second, jnp.where(pos >= first, first, 0))

    for piece in range(count):
        q_all[pl.ds(piece * 2 * sec, 2 * sec), :] = q_refs[piece][...]

    def one_section(index, _):
        piece, part = index // 2, lax.rem(index, 2)
        shift = shifts[0]
        for i in range(1, count):
            shift = jnp.where(piece == i, shifts[i], shift)
        section = ((zl * RING + x) * RING + wrap(y + shift)) * 2 + part
        place = table[section]
        begin = place * sec
        own_rows = pl.ds(pl.multiple_of(index * sec, ROW_TILE), sec)

        @pl.when(table[nsec + place] == 0)
        def _():
            out_all[own_rows, :] = jnp.zeros((sec, groups * HD), out_all.dtype)

        @pl.when(table[nsec + place] != 0)
        def _():
            key_first = segment_start(begin) // ROW_TILE * ROW_TILE
            last_start = segment_start(begin + sec - 1)
            full = (begin + sec - key_first) // BLOCK_KEYS
            tail_first = key_first + full * BLOCK_KEYS
            tail_steps = (begin + sec - tail_first + TAIL_STEP - 1) // TAIL_STEP
            peak[...] = jnp.full(peak.shape, -1e30, jnp.float32)
            acc[...] = jnp.zeros(acc.shape, jnp.float32)

            def step(first, width, masked):
                at = pl.multiple_of(first, ROW_TILE)
                keys = held[pl.ds(at, width), pl.ds(0, HD)]
                values = held[pl.ds(at, width), pl.ds(HD, 2 * HD)]
                if masked:
                    row_pos = begin + lax.broadcasted_iota(jnp.int32, (sec, 1), 0)
                    row_start = segment_start(row_pos)
                    key_pos = at + lax.broadcasted_iota(jnp.int32, (1, width), 1)
                    seen = (key_pos <= row_pos) & (key_pos >= row_start)
                def score(g):
                    got = lax.dot_general(
                        q_all[own_rows, pl.ds(g * HD, HD)],
                        keys,
                        (((1,), (1,)), ((), ())),
                        preferred_element_type=jnp.float32,
                    )
                    return jnp.where(seen, got, -1e30) if masked else got

                def weigh(g, got):
                    rows_g = pl.ds(g * sec, sec)
                    before = peak[rows_g, :]
                    top = jnp.maximum(before, jnp.max(got, axis=1, keepdims=True))
                    peak[rows_g, :] = top
                    scaled = top * factor
                    weights = jnp.exp2(
                        got * factor - jnp.concatenate([scaled] * (width // HD), axis=1)
                    ).astype(jnp.bfloat16)
                    return weights, jnp.exp2(before * factor - scaled)

                def add(g, weights, rescale):
                    rows_g = pl.ds(g * sec, sec)
                    acc[rows_g, :] = acc[rows_g, :] * jnp.concatenate(
                        [rescale, rescale], axis=1
                    ) + jnp.dot(weights, values, preferred_element_type=jnp.float32)

                ahead = score(0)
                waiting = None
                for g in range(groups):
                    got, ahead = ahead, score(g + 1) if g + 1 < groups else None
                    if waiting is not None:
                        add(g - 1, *waiting)
                    waiting = weigh(g, got)
                add(groups - 1, *waiting)

            def full_block(block, _):
                first = key_first + block * BLOCK_KEYS
                masked = (first < last_start) | (first + BLOCK_KEYS > begin)
                pl.when(masked)(lambda: step(first, BLOCK_KEYS, True))
                pl.when(jnp.logical_not(masked))(lambda: step(first, BLOCK_KEYS, False))
                return 0

            lax.fori_loop(0, full, full_block, 0)
            for steps in range(1, BLOCK_KEYS // TAIL_STEP + 1):
                pl.when(tail_steps == steps)(
                    lambda steps=steps: step(tail_first, steps * TAIL_STEP, True)
                )
            for g in range(groups):
                rows_g = pl.ds(g * sec, sec)
                out_all[own_rows, pl.ds(g * HD, HD)] = (
                    acc[rows_g, pl.ds(0, HD)] / acc[rows_g, pl.ds(HD, HD)]
                ).astype(out_all.dtype)

        return 0

    lax.fori_loop(0, 2 * count, one_section, 0)
    for piece in range(count):
        out_refs[piece][...] = out_all[pl.ds(piece * 2 * sec, 2 * sec), :]


def attention(table, shifts, q_pieces, kv_pieces, sec, nsec):
    groups = q_pieces[0].shape[1] // HD
    rows = nsec * sec
    count = len(shifts)
    smem = pl.BlockSpec(memory_space=pltpu.SMEM)
    vmem = pl.BlockSpec(memory_space=pltpu.VMEM)
    return pl.pallas_call(
        functools.partial(attention_kernel, groups, sec, nsec, shifts),
        out_shape=[jax.ShapeDtypeStruct(q.shape, q.dtype) for q in q_pieces],
        in_specs=[smem] + [vmem] * count + [pl.BlockSpec(memory_space=pl.ANY)] * 9,
        out_specs=[vmem] * count,
        scratch_shapes=[
            pltpu.VMEM((rows + TAIL_STEP, 3 * HD), jnp.bfloat16),
            pltpu.VMEM((2 * count * sec, groups * HD), jnp.bfloat16),
            pltpu.VMEM((2 * count * sec, groups * HD), jnp.bfloat16),
            pltpu.VMEM((groups * sec, 2 * HD), jnp.float32),
            pltpu.VMEM((groups * sec, HD), jnp.float32),
            pltpu.SemaphoreType.DMA,
        ],
        compiler_params=pltpu.CompilerParams(vmem_limit_bytes=48 * 2**20),
        cost_estimate=pl.CostEstimate(
            flops=count * 2 * 10**9,
            bytes_accessed=6 * 10**6,
            transcendentals=count * 4 * 10**6,
        ),
        name="attend",
    )(table, *q_pieces, *kv_pieces)


def project_kernel(base, table, *refs):
    att_refs, weights = refs[:8], refs[8]
    own_out, other_out, att = refs[9:]
    tok, wide = att_refs[0].shape

    @pl.when(pl.program_id(0) == 0)
    def _():
        for who in range(2):
            for j in range(4):
                head = wrap(table[base + 4] + SHIFTS[j])
                at = pl.multiple_of(head * wide, HD)
                att[pl.ds(who * tok, tok), pl.ds(at, wide)] = att_refs[4 * who + j][...]

    got = jnp.dot(att[...], weights[...], preferred_element_type=jnp.float32)
    got = got.astype(own_out.dtype)
    own_out[...] = got[:tok]
    other_out[0] = got[tok:]


def project(table, base, own_att, other_att, weights):
    tok, wide = own_att[0].shape
    rows, cols = RING * wide, weights.shape[1]
    piece = pl.BlockSpec((tok, wide), lambda i, *_: (0, 0))
    return pl.pallas_call(
        functools.partial(project_kernel, base),
        out_shape=[
            jax.ShapeDtypeStruct((tok, 4 * cols), jnp.bfloat16),
            jax.ShapeDtypeStruct((2, tok, cols), jnp.bfloat16),
        ],
        grid_spec=pltpu.PrefetchScalarGridSpec(
            num_scalar_prefetch=1,
            grid=(2,),
            in_specs=[piece] * 8 + [pl.BlockSpec((rows, cols), lambda i, *_: (i, 0))],
            out_specs=[
                pl.BlockSpec((tok, cols), lambda i, table: (0, i * 2 + table[base + 6])),
                pl.BlockSpec((1, tok, cols), lambda i, *_: (i, 0, 0)),
            ],
            scratch_shapes=[pltpu.VMEM((2 * tok, rows), jnp.bfloat16)],
        ),
        compiler_params=pltpu.CompilerParams(vmem_limit_bytes=48 * 2**20),
        cost_estimate=pl.CostEstimate(
            flops=6 * 10**9, bytes_accessed=18 * 10**6, transcendentals=0
        ),
        name="project",
    )(table, *own_att, *other_att, weights)


def merge_kernel(base, table, theirs, whole, out, sems):
    del whole
    cols = theirs.shape[2]

    def store(half):
        at = pl.multiple_of((half * 2 + 1 - table[base + 6]) * cols, HD)
        return pltpu.make_async_copy(theirs.at[half], out.at[:, pl.ds(at, cols)], sems.at[half])

    for half in range(2):
        store(half).start()
    for half in range(2):
        store(half).wait()


def merge(table, base, theirs, whole):
    anywhere = pl.BlockSpec(memory_space=pl.ANY)
    return pl.pallas_call(
        functools.partial(merge_kernel, base),
        out_shape=jax.ShapeDtypeStruct(whole.shape, whole.dtype),
        in_specs=[
            pl.BlockSpec(memory_space=pltpu.SMEM),
            pl.BlockSpec(memory_space=pltpu.VMEM),
            anywhere,
        ],
        out_specs=anywhere,
        scratch_shapes=[pltpu.SemaphoreType.DMA((2,))],
        input_output_aliases={2: 0},
        cost_estimate=pl.CostEstimate(flops=0, bytes_accessed=3 * 10**6, transcendentals=0),
        name="merge",
    )(table, theirs, whole)


def per_device(query, keys, values, section_order, kept_sections, segment_ids, out_weight):
    tok = query.shape[1]
    sec = tok // 2
    nsec = section_order.shape[0]
    zh, core = lax.axis_index("zh"), lax.axis_index("c")
    zl, x, y = lax.axis_index("zl"), lax.axis_index("x"), lax.axis_index("y")
    first, second = jnp.sum(segment_ids[0] < 1), jnp.sum(segment_ids[0] < 2)
    scalars = jnp.stack([first, second, zl, x, y, zh * 2 + zl, core]).astype(jnp.int32)
    table = jnp.concatenate([section_order, kept_sections[0], scalars])

    def head_slice(array, shift):
        wide = array.shape[2] // RING
        return lax.dynamic_slice_in_dim(array[0], wrap(y + shift) * wide, wide, 1)

    weights = lax.all_gather(out_weight, ("zh", "zl", "x", "y"), axis=0, tiled=True)

    pieces, q_pieces = [], []
    for shift in SHIFTS:
        kv = jnp.concatenate([head_slice(keys, -shift), head_slice(values, -shift)], axis=1)
        pieces.append(kv if shift == 0 else shifted(kv, "y", -shift))
    for shift in SHIFTS:
        q = head_slice(query, -shift)
        q_pieces.append(q if shift == 0 else shifted(q, "y", -shift))
    own = jnp.stack(pieces)
    far = shifted(own, "zl", 1, 2)
    near = ring_gather(own, "x")
    opposite = jnp.concatenate([near[3], near[4]], axis=0)
    far_all = (far, shifted(far, "x", 1), shifted(far, "x", -1), shifted(opposite, "zl", 1, 2))
    attended = attention(table, SHIFTS, q_pieces, near + far_all, sec, nsec)

    by_shift = dict(zip(SHIFTS, attended))
    back = {0: by_shift[0]}
    for shift in SHIFTS[1:]:
        back[wrap_static(-shift)] = shifted(by_shift[shift], "y", shift)
    own_att = [back[s] for s in SHIFTS]
    other_att = [shifted(a, "c", 1, 2) for a in own_att]
    base = 2 * nsec
    whole, for_other = project(table, base, own_att, other_att, weights)
    return merge(table, base, shifted(for_other, "c", 1, 2), whole)[None]


def wrap_static(shift):
    return 2 if shift in (2, -2) else shift


def solution(mesh):
    fine = Mesh(mesh.devices.reshape(2, 2, 2, 4, 4), ("zh", "c", "zl", "x", "y"))
    dp, ctx = ("zh", "c"), ("zl", "x", "y")
    return jax.shard_map(
        per_device,
        mesh=fine,
        in_specs=(
            P(dp, ctx, None),
            P(dp, ctx, None),
            P(dp, ctx, None),
            P(),
            P(dp, None),
            P(dp, None),
            P(ctx, dp),
        ),
        out_specs=P(dp, ctx, None),
        check_vma=False,
    )
```

```python
import functools
import math

import jax
import jax.numpy as jnp
from jax import lax
from jax.experimental import pallas as pl
from jax.experimental.pallas import tpu as pltpu
from jax.sharding import Mesh, PartitionSpec as P

HD = 128
RING = 4
SHIFTS = (0, -1, 1, 2)
BLOCK_KEYS = 2048
TAIL_STEP = 256
CHUNK = 256
ROW_TILE = 16


def shifted(array, axis, step, size=RING):
    return lax.ppermute(array, axis, [(i, (i + step) % size) for i in range(size)])


def ring_gather(array, axis):
    half = array.shape[0] // 2
    from_left = shifted(array, axis, 1)
    from_right = shifted(array, axis, -1)
    far_head = shifted(from_left[:half], axis, 1)
    far_tail = shifted(from_right[half:], axis, -1)
    return array, from_left, from_right, far_head, far_tail


def wrap(value):
    return lax.rem(value + RING, RING)


def attention_kernel(
    groups, sec, nsec, shifts, table, *refs
):
    count = len(shifts)
    q_refs, kv_refs, out_refs = refs[:count], refs[count : count + 9], refs[count + 9 : 2 * count + 9]
    held, q_all, out_all, acc, peak, sem = refs[2 * count + 9 :]
    base = 2 * nsec
    zl, x, y = table[base + 2], table[base + 3], table[base + 4]
    rows = nsec * sec
    factor = math.log2(math.e) / math.sqrt(HD)

    def copies(act):
        for side in range(2):
            own_zl = zl if side == 0 else 1 - zl
            for x_rel in range(4):
                abs_x = wrap(x + SHIFTS[x_rel])
                for y_rel in range(4):
                    abs_y = wrap(y + SHIFTS[y_rel])
                    if side == 1:
                        source = kv_refs[5 + x_rel].at[y_rel]
                    elif x_rel < 3:
                        source = kv_refs[x_rel].at[y_rel]
                    else:
                        source = kv_refs[3 + y_rel // 2].at[y_rel % 2]
                    for part in range(2):
                        section = ((own_zl * RING + abs_x) * RING + abs_y) * 2 + part
                        at = pl.multiple_of(table[section] * sec, ROW_TILE)
                        act(
                            source.at[pl.ds(part * sec, sec), :],
                            held.at[pl.ds(at, sec), pl.ds(0, 2 * HD)],
                        )

    copies(lambda a, b: pltpu.make_async_copy(a, b, sem).start())
    pad = held.shape[0] - rows
    held[pl.ds(rows, pad), pl.ds(0, 2 * HD)] = jnp.zeros((pad, 2 * HD), held.dtype)
    held[:, pl.ds(2 * HD, HD)] = jnp.ones((held.shape[0], HD), held.dtype)
    copies(lambda a, b: pltpu.make_async_copy(a, b, sem).wait())

    first, second = table[base], table[base + 1]

    def segment_start(pos):
        return jnp.where(pos >= second, second, jnp.where(pos >= first, first, 0))

    for piece in range(count):
        q_all[pl.ds(piece * 2 * sec, 2 * sec), :] = q_refs[piece][...]

    def one_section(index, _):
        piece, part = index // 2, lax.rem(index, 2)
        shift = shifts[0]
        for i in range(1, count):
            shift = jnp.where(piece == i, shifts[i], shift)
        section = ((zl * RING + x) * RING + wrap(y + shift)) * 2 + part
        place = table[section]
        begin = place * sec
        own_rows = pl.ds(pl.multiple_of(index * sec, ROW_TILE), sec)

        @pl.when(table[nsec + place] == 0)
        def _():
            out_all[own_rows, :] = jnp.zeros((sec, groups * HD), out_all.dtype)

        @pl.when(table[nsec + place] != 0)
        def _():
            key_first = segment_start(begin) // ROW_TILE * ROW_TILE
            last_start = segment_start(begin + sec - 1)
            full = (begin + sec - key_first) // BLOCK_KEYS
            tail_first = key_first + full * BLOCK_KEYS
            tail_steps = (begin + sec - tail_first + TAIL_STEP - 1) // TAIL_STEP
            peak[...] = jnp.full(peak.shape, -1e30, jnp.float32)
            acc[...] = jnp.zeros(acc.shape, jnp.float32)

            def step(first, width, masked):
                at = pl.multiple_of(first, ROW_TILE)
                keys = held[pl.ds(at, width), pl.ds(0, HD)]
                values = held[pl.ds(at, width), pl.ds(HD, 2 * HD)]
                if masked:
                    row_pos = begin + lax.broadcasted_iota(jnp.int32, (sec, 1), 0)
                    row_start = segment_start(row_pos)
                    key_pos = at + lax.broadcasted_iota(jnp.int32, (1, width), 1)
                    seen = (key_pos <= row_pos) & (key_pos >= row_start)
                def score(g):
                    got = lax.dot_general(
                        q_all[own_rows, pl.ds(g * HD, HD)],
                        keys,
                        (((1,), (1,)), ((), ())),
                        preferred_element_type=jnp.float32,
                    )
                    return jnp.where(seen, got, -1e30) if masked else got

                def weigh(g, got):
                    rows_g = pl.ds(g * sec, sec)
                    before = peak[rows_g, :]
                    top = jnp.maximum(before, jnp.max(got, axis=1, keepdims=True))
                    peak[rows_g, :] = top
                    scaled = top * factor
                    weights = jnp.exp2(
                        got * factor - jnp.concatenate([scaled] * (width // HD), axis=1)
                    ).astype(jnp.bfloat16)
                    return weights, jnp.exp2(before * factor - scaled)

                def add(g, weights, rescale):
                    rows_g = pl.ds(g * sec, sec)
                    acc[rows_g, :] = acc[rows_g, :] * jnp.concatenate(
                        [rescale, rescale], axis=1
                    ) + jnp.dot(weights, values, preferred_element_type=jnp.float32)

                ahead = score(0)
                waiting = None
                for g in range(groups):
                    got, ahead = ahead, score(g + 1) if g + 1 < groups else None
                    if waiting is not None:
                        add(g - 1, *waiting)
                    waiting = weigh(g, got)
                add(groups - 1, *waiting)

            def full_block(block, _):
                first = key_first + block * BLOCK_KEYS
                masked = (first < last_start) | (first + BLOCK_KEYS > begin)
                pl.when(masked)(lambda: step(first, BLOCK_KEYS, True))
                pl.when(jnp.logical_not(masked))(lambda: step(first, BLOCK_KEYS, False))
                return 0

            lax.fori_loop(0, full, full_block, 0)
            for steps in range(1, BLOCK_KEYS // TAIL_STEP + 1):
                pl.when(tail_steps == steps)(
                    lambda steps=steps: step(tail_first, steps * TAIL_STEP, True)
                )
            for g in range(groups):
                rows_g = pl.ds(g * sec, sec)
                out_all[own_rows, pl.ds(g * HD, HD)] = (
                    acc[rows_g, pl.ds(0, HD)] / acc[rows_g, pl.ds(HD, HD)]
                ).astype(out_all.dtype)

        return 0

    lax.fori_loop(0, 2 * count, one_section, 0)
    for piece in range(count):
        out_refs[piece][...] = out_all[pl.ds(piece * 2 * sec, 2 * sec), :]


def attention(table, shifts, q_pieces, kv_pieces, sec, nsec):
    groups = q_pieces[0].shape[1] // HD
    rows = nsec * sec
    count = len(shifts)
    smem = pl.BlockSpec(memory_space=pltpu.SMEM)
    vmem = pl.BlockSpec(memory_space=pltpu.VMEM)
    return pl.pallas_call(
        functools.partial(attention_kernel, groups, sec, nsec, shifts),
        out_shape=[jax.ShapeDtypeStruct(q.shape, q.dtype) for q in q_pieces],
        in_specs=[smem] + [vmem] * count + [pl.BlockSpec(memory_space=pl.ANY)] * 9,
        out_specs=[vmem] * count,
        scratch_shapes=[
            pltpu.VMEM((rows + TAIL_STEP, 3 * HD), jnp.bfloat16),
            pltpu.VMEM((2 * count * sec, groups * HD), jnp.bfloat16),
            pltpu.VMEM((2 * count * sec, groups * HD), jnp.bfloat16),
            pltpu.VMEM((groups * sec, 2 * HD), jnp.float32),
            pltpu.VMEM((groups * sec, HD), jnp.float32),
            pltpu.SemaphoreType.DMA,
        ],
        compiler_params=pltpu.CompilerParams(vmem_limit_bytes=48 * 2**20),
        cost_estimate=pl.CostEstimate(
            flops=count * 2 * 10**9,
            bytes_accessed=6 * 10**6,
            transcendentals=count * 4 * 10**6,
        ),
        name="attend",
    )(table, *q_pieces, *kv_pieces)


def project_kernel(*refs):
    att_refs, weights = refs[:8], refs[8]
    whole, other_out, att, held, own, sems = refs[9:]
    tok, wide = att_refs[0].shape
    cols = weights.shape[1]
    rows = RING * wide
    chunks = cols // CHUNK
    y, core = lax.axis_index("y"), lax.axis_index("c")

    def load(half, i):
        at = (pl.ds(half * rows, rows), pl.ds(i * CHUNK, CHUNK))
        return pltpu.make_async_copy(weights.at[at], held.at[at], sems.at[half * chunks + i])

    def store(half):
        at = pl.multiple_of((half * 2 + core) * cols, HD)
        return pltpu.make_async_copy(
            own.at[half], whole.at[:, pl.ds(at, cols)], sems.at[2 * chunks + half]
        )

    for half in range(2):
        for i in range(chunks):
            load(half, i).start()
    for who in range(2):
        for j in range(4):
            at = pl.multiple_of(wrap(y + SHIFTS[j]) * wide, HD)
            att[pl.ds(who * tok, tok), pl.ds(at, wide)] = att_refs[4 * who + j][...]
    for half in range(2):
        for i in range(chunks):
            load(half, i).wait()
            at = pl.ds(i * CHUNK, CHUNK)
            got = jnp.dot(
                att[...], held[pl.ds(half * rows, rows), at], preferred_element_type=jnp.float32
            ).astype(own.dtype)
            own[half, :, at] = got[:tok]
            other_out[half, :, at] = got[tok:]
        store(half).start()
    for half in range(2):
        store(half).wait()


def project(own_att, other_att, weights):
    tok, wide = own_att[0].shape
    rows, cols = RING * wide, weights.shape[1]
    vmem = pl.BlockSpec(memory_space=pltpu.VMEM)
    anywhere = pl.BlockSpec(memory_space=pl.ANY)
    return pl.pallas_call(
        project_kernel,
        out_shape=[
            jax.ShapeDtypeStruct((tok, 4 * cols), jnp.bfloat16),
            jax.ShapeDtypeStruct((2, tok, cols), jnp.bfloat16),
        ],
        in_specs=[vmem] * 8 + [anywhere],
        out_specs=[anywhere, vmem],
        scratch_shapes=[
            pltpu.VMEM((2 * tok, rows), jnp.bfloat16),
            pltpu.VMEM((2 * rows, cols), jnp.bfloat16),
            pltpu.VMEM((2, tok, cols), jnp.bfloat16),
            pltpu.SemaphoreType.DMA((2 * cols // CHUNK + 2,)),
        ],
        compiler_params=pltpu.CompilerParams(vmem_limit_bytes=48 * 2**20),
        cost_estimate=pl.CostEstimate(
            flops=6 * 10**9, bytes_accessed=18 * 10**6, transcendentals=0
        ),
        name="project",
    )(*own_att, *other_att, weights)


def merge_kernel(theirs, whole, out, sems):
    del whole
    cols = theirs.shape[2]
    core = lax.axis_index("c")

    def store(half):
        at = pl.multiple_of((half * 2 + 1 - core) * cols, HD)
        return pltpu.make_async_copy(theirs.at[half], out.at[:, pl.ds(at, cols)], sems.at[half])

    for half in range(2):
        store(half).start()
    for half in range(2):
        store(half).wait()


def merge(theirs, whole):
    anywhere = pl.BlockSpec(memory_space=pl.ANY)
    return pl.pallas_call(
        merge_kernel,
        out_shape=jax.ShapeDtypeStruct(whole.shape, whole.dtype),
        in_specs=[pl.BlockSpec(memory_space=pltpu.VMEM), anywhere],
        out_specs=anywhere,
        scratch_shapes=[pltpu.SemaphoreType.DMA((2,))],
        input_output_aliases={1: 0},
        cost_estimate=pl.CostEstimate(flops=0, bytes_accessed=3 * 10**6, transcendentals=0),
        name="merge",
    )(theirs, whole)


def per_device(query, keys, values, section_order, kept_sections, segment_ids, out_weight):
    tok = query.shape[1]
    sec = tok // 2
    nsec = section_order.shape[0]
    zl, x, y = lax.axis_index("zl"), lax.axis_index("x"), lax.axis_index("y")
    first, second = jnp.sum(segment_ids[0] < 1), jnp.sum(segment_ids[0] < 2)
    scalars = jnp.stack([first, second, zl, x, y]).astype(jnp.int32)
    table = jnp.concatenate([section_order, kept_sections[0], scalars])

    def head_slice(array, shift):
        wide = array.shape[2] // RING
        return lax.dynamic_slice_in_dim(array[0], wrap(y + shift) * wide, wide, 1)

    weights = lax.all_gather(out_weight, ("zh", "zl", "x", "y"), axis=0, tiled=True)

    pieces, q_pieces = [], []
    for shift in SHIFTS:
        kv = jnp.concatenate([head_slice(keys, -shift), head_slice(values, -shift)], axis=1)
        pieces.append(kv if shift == 0 else shifted(kv, "y", -shift))
    for shift in SHIFTS:
        q = head_slice(query, -shift)
        q_pieces.append(q if shift == 0 else shifted(q, "y", -shift))
    own = jnp.stack(pieces)
    far = shifted(own, "zl", 1, 2)
    near = ring_gather(own, "x")
    opposite = jnp.concatenate([near[3], near[4]], axis=0)
    far_all = (far, shifted(far, "x", 1), shifted(far, "x", -1), shifted(opposite, "zl", 1, 2))
    attended = attention(table, SHIFTS, q_pieces, near + far_all, sec, nsec)

    by_shift = dict(zip(SHIFTS, attended))
    back = {0: by_shift[0]}
    for shift in SHIFTS[1:]:
        back[wrap_static(-shift)] = shifted(by_shift[shift], "y", shift)
    own_att = [back[s] for s in SHIFTS]
    other_att = [shifted(a, "c", 1, 2) for a in own_att]
    whole, for_other = project(own_att, other_att, weights)
    return merge(shifted(for_other, "c", 1, 2), whole)[None]


def wrap_static(shift):
    return 2 if shift in (2, -2) else shift


def solution(mesh):
    fine = Mesh(mesh.devices.reshape(2, 2, 2, 4, 4), ("zh", "c", "zl", "x", "y"))
    dp, ctx = ("zh", "c"), ("zl", "x", "y")
    return jax.shard_map(
        per_device,
        mesh=fine,
        in_specs=(
            P(dp, ctx, None),
            P(dp, ctx, None),
            P(dp, ctx, None),
            P(),
            P(dp, None),
            P(dp, None),
            P(ctx, dp),
        ),
        out_specs=P(dp, ctx, None),
        check_vma=False,
    )
```

```python
import functools
import math

import jax
import jax.numpy as jnp
from jax import lax
from jax.experimental import pallas as pl
from jax.experimental.pallas import tpu as pltpu
from jax.sharding import Mesh, PartitionSpec as P

HD = 128
RING = 4
SHIFTS = (0, -1, 1, 2)
BLOCK_KEYS = 2048
TAIL_STEP = 256
ROW_TILE = 16


def shifted(array, axis, step, size=RING):
    return lax.ppermute(array, axis, [(i, (i + step) % size) for i in range(size)])


def ring_gather(array, axis):
    half = array.shape[0] // 2
    from_left = shifted(array, axis, 1)
    from_right = shifted(array, axis, -1)
    far_head = shifted(from_left[:half], axis, 1)
    far_tail = shifted(from_right[half:], axis, -1)
    return array, from_left, from_right, far_head, far_tail


def wrap(value):
    return lax.rem(value + RING, RING)


def attention_kernel(
    groups, sec, nsec, shifts, table, *refs
):
    count = len(shifts)
    q_refs, kv_refs, out_refs = refs[:count], refs[count : count + 9], refs[count + 9 : 2 * count + 9]
    held, q_all, out_all, acc, peak, sem = refs[2 * count + 9 :]
    base = 2 * nsec
    zl, x, y = table[base + 2], table[base + 3], table[base + 4]
    rows = nsec * sec
    factor = math.log2(math.e) / math.sqrt(HD)

    def copies(act):
        for side in range(2):
            own_zl = zl if side == 0 else 1 - zl
            for x_rel in range(4):
                abs_x = wrap(x + SHIFTS[x_rel])
                for y_rel in range(4):
                    abs_y = wrap(y + SHIFTS[y_rel])
                    if side == 1:
                        source = kv_refs[5 + x_rel].at[y_rel]
                    elif x_rel < 3:
                        source = kv_refs[x_rel].at[y_rel]
                    else:
                        source = kv_refs[3 + y_rel // 2].at[y_rel % 2]
                    for part in range(2):
                        section = ((own_zl * RING + abs_x) * RING + abs_y) * 2 + part
                        at = pl.multiple_of(table[section] * sec, ROW_TILE)
                        act(
                            source.at[pl.ds(part * sec, sec), :],
                            held.at[pl.ds(at, sec), pl.ds(0, 2 * HD)],
                        )

    copies(lambda a, b: pltpu.make_async_copy(a, b, sem).start())
    pad = held.shape[0] - rows
    held[pl.ds(rows, pad), pl.ds(0, 2 * HD)] = jnp.zeros((pad, 2 * HD), held.dtype)
    held[:, pl.ds(2 * HD, HD)] = jnp.ones((held.shape[0], HD), held.dtype)
    copies(lambda a, b: pltpu.make_async_copy(a, b, sem).wait())

    first, second = table[base], table[base + 1]

    def segment_start(pos):
        return jnp.where(pos >= second, second, jnp.where(pos >= first, first, 0))

    for piece in range(count):
        q_all[pl.ds(piece * 2 * sec, 2 * sec), :] = q_refs[piece][...]

    def one_section(index, _):
        piece, part = index // 2, lax.rem(index, 2)
        shift = shifts[0]
        for i in range(1, count):
            shift = jnp.where(piece == i, shifts[i], shift)
        section = ((zl * RING + x) * RING + wrap(y + shift)) * 2 + part
        place = table[section]
        begin = place * sec
        own_rows = pl.ds(pl.multiple_of(index * sec, ROW_TILE), sec)

        @pl.when(table[nsec + place] == 0)
        def _():
            out_all[own_rows, :] = jnp.zeros((sec, groups * HD), out_all.dtype)

        @pl.when(table[nsec + place] != 0)
        def _():
            key_first = segment_start(begin) // ROW_TILE * ROW_TILE
            last_start = segment_start(begin + sec - 1)
            full = (begin + sec - key_first) // BLOCK_KEYS
            tail_first = key_first + full * BLOCK_KEYS
            tail_steps = (begin + sec - tail_first + TAIL_STEP - 1) // TAIL_STEP
            peak[...] = jnp.full(peak.shape, -1e30, jnp.float32)
            acc[...] = jnp.zeros(acc.shape, jnp.float32)

            def step(first, width, masked):
                at = pl.multiple_of(first, ROW_TILE)
                keys = held[pl.ds(at, width), pl.ds(0, HD)]
                values = held[pl.ds(at, width), pl.ds(HD, 2 * HD)]
                if masked:
                    row_pos = begin + lax.broadcasted_iota(jnp.int32, (sec, 1), 0)
                    row_start = segment_start(row_pos)
                    key_pos = at + lax.broadcasted_iota(jnp.int32, (1, width), 1)
                    seen = (key_pos <= row_pos) & (key_pos >= row_start)
                def score(g):
                    got = lax.dot_general(
                        q_all[own_rows, pl.ds(g * HD, HD)],
                        keys,
                        (((1,), (1,)), ((), ())),
                        preferred_element_type=jnp.float32,
                    )
                    return jnp.where(seen, got, -1e30) if masked else got

                def weigh(g, got):
                    rows_g = pl.ds(g * sec, sec)
                    before = peak[rows_g, :]
                    top = jnp.maximum(before, jnp.max(got, axis=1, keepdims=True))
                    peak[rows_g, :] = top
                    scaled = top * factor
                    weights = jnp.exp2(
                        got * factor - jnp.concatenate([scaled] * (width // HD), axis=1)
                    ).astype(jnp.bfloat16)
                    return weights, jnp.exp2(before * factor - scaled)

                def add(g, weights, rescale):
                    rows_g = pl.ds(g * sec, sec)
                    acc[rows_g, :] = acc[rows_g, :] * jnp.concatenate(
                        [rescale, rescale], axis=1
                    ) + jnp.dot(weights, values, preferred_element_type=jnp.float32)

                ahead = score(0)
                waiting = None
                for g in range(groups):
                    got, ahead = ahead, score(g + 1) if g + 1 < groups else None
                    if waiting is not None:
                        add(g - 1, *waiting)
                    waiting = weigh(g, got)
                add(groups - 1, *waiting)

            def full_block(block, _):
                first = key_first + block * BLOCK_KEYS
                masked = (first < last_start) | (first + BLOCK_KEYS > begin)
                pl.when(masked)(lambda: step(first, BLOCK_KEYS, True))
                pl.when(jnp.logical_not(masked))(lambda: step(first, BLOCK_KEYS, False))
                return 0

            lax.fori_loop(0, full, full_block, 0)
            for steps in range(1, BLOCK_KEYS // TAIL_STEP + 1):
                pl.when(tail_steps == steps)(
                    lambda steps=steps: step(tail_first, steps * TAIL_STEP, True)
                )
            for g in range(groups):
                rows_g = pl.ds(g * sec, sec)
                out_all[own_rows, pl.ds(g * HD, HD)] = (
                    acc[rows_g, pl.ds(0, HD)] / acc[rows_g, pl.ds(HD, HD)]
                ).astype(out_all.dtype)

        return 0

    lax.fori_loop(0, 2 * count, one_section, 0)
    for piece in range(count):
        out_refs[piece][...] = out_all[pl.ds(piece * 2 * sec, 2 * sec), :]


def attention(table, shifts, q_pieces, kv_pieces, sec, nsec):
    groups = q_pieces[0].shape[1] // HD
    rows = nsec * sec
    count = len(shifts)
    smem = pl.BlockSpec(memory_space=pltpu.SMEM)
    vmem = pl.BlockSpec(memory_space=pltpu.VMEM)
    return pl.pallas_call(
        functools.partial(attention_kernel, groups, sec, nsec, shifts),
        out_shape=[jax.ShapeDtypeStruct(q.shape, q.dtype) for q in q_pieces],
        in_specs=[smem] + [vmem] * count + [pl.BlockSpec(memory_space=pl.ANY)] * 9,
        out_specs=[vmem] * count,
        scratch_shapes=[
            pltpu.VMEM((rows + TAIL_STEP, 3 * HD), jnp.bfloat16),
            pltpu.VMEM((2 * count * sec, groups * HD), jnp.bfloat16),
            pltpu.VMEM((2 * count * sec, groups * HD), jnp.bfloat16),
            pltpu.VMEM((groups * sec, 2 * HD), jnp.float32),
            pltpu.VMEM((groups * sec, HD), jnp.float32),
            pltpu.SemaphoreType.DMA,
        ],
        compiler_params=pltpu.CompilerParams(vmem_limit_bytes=24 * 2**20),
        cost_estimate=pl.CostEstimate(
            flops=count * 2 * 10**9,
            bytes_accessed=6 * 10**6,
            transcendentals=count * 4 * 10**6,
        ),
        name="attend",
    )(table, *q_pieces, *kv_pieces)


def project_kernel(base, table, *refs):
    att_refs, weights = refs[:8], refs[8]
    own_out, other_out, att = refs[9:]
    tok, wide = att_refs[0].shape

    @pl.when(pl.program_id(0) == 0)
    def _():
        for who in range(2):
            for j in range(4):
                head = wrap(table[base + 4] + SHIFTS[j])
                at = pl.multiple_of(head * wide, HD)
                att[pl.ds(who * tok, tok), pl.ds(at, wide)] = att_refs[4 * who + j][...]

    got = jnp.dot(att[...], weights[...], preferred_element_type=jnp.float32)
    got = got.astype(own_out.dtype)
    own_out[...] = got[:tok]
    other_out[0] = got[tok:]


def project(table, base, own_att, other_att, weights):
    tok, wide = own_att[0].shape
    rows, cols = RING * wide, weights.shape[1]
    piece = pl.BlockSpec((tok, wide), lambda i, *_: (0, 0))
    return pl.pallas_call(
        functools.partial(project_kernel, base),
        out_shape=[
            jax.ShapeDtypeStruct((tok, 4 * cols), jnp.bfloat16),
            jax.ShapeDtypeStruct((2, tok, cols), jnp.bfloat16),
        ],
        grid_spec=pltpu.PrefetchScalarGridSpec(
            num_scalar_prefetch=1,
            grid=(2,),
            in_specs=[piece] * 8 + [pl.BlockSpec((rows, cols), lambda i, *_: (i, 0))],
            out_specs=[
                pl.BlockSpec((tok, cols), lambda i, table: (0, i * 2 + table[base + 6])),
                pl.BlockSpec((1, tok, cols), lambda i, *_: (i, 0, 0)),
            ],
            scratch_shapes=[pltpu.VMEM((2 * tok, rows), jnp.bfloat16)],
        ),
        compiler_params=pltpu.CompilerParams(vmem_limit_bytes=32 * 2**20),
        cost_estimate=pl.CostEstimate(
            flops=6 * 10**9, bytes_accessed=18 * 10**6, transcendentals=0
        ),
        name="project",
    )(table, *own_att, *other_att, weights)


def merge_kernel(base, table, theirs, whole, out, sems):
    del whole
    cols = theirs.shape[2]

    def store(half):
        at = pl.multiple_of((half * 2 + 1 - table[base + 6]) * cols, HD)
        return pltpu.make_async_copy(theirs.at[half], out.at[:, pl.ds(at, cols)], sems.at[half])

    for half in range(2):
        store(half).start()
    for half in range(2):
        store(half).wait()


def merge(table, base, theirs, whole):
    anywhere = pl.BlockSpec(memory_space=pl.ANY)
    return pl.pallas_call(
        functools.partial(merge_kernel, base),
        out_shape=jax.ShapeDtypeStruct(whole.shape, whole.dtype),
        in_specs=[
            pl.BlockSpec(memory_space=pltpu.SMEM),
            pl.BlockSpec(memory_space=pltpu.VMEM),
            anywhere,
        ],
        out_specs=anywhere,
        scratch_shapes=[pltpu.SemaphoreType.DMA((2,))],
        input_output_aliases={2: 0},
        compiler_params=pltpu.CompilerParams(vmem_limit_bytes=8 * 2**20),
        cost_estimate=pl.CostEstimate(flops=0, bytes_accessed=3 * 10**6, transcendentals=0),
        name="merge",
    )(table, theirs, whole)


def per_device(query, keys, values, section_order, kept_sections, segment_ids, out_weight):
    tok = query.shape[1]
    sec = tok // 2
    nsec = section_order.shape[0]
    zh, core = lax.axis_index("zh"), lax.axis_index("c")
    zl, x, y = lax.axis_index("zl"), lax.axis_index("x"), lax.axis_index("y")
    first, second = jnp.sum(segment_ids[0] < 1), jnp.sum(segment_ids[0] < 2)
    scalars = jnp.stack([first, second, zl, x, y, zh * 2 + zl, core]).astype(jnp.int32)
    table = jnp.concatenate([section_order, kept_sections[0], scalars])

    def head_slice(array, shift):
        wide = array.shape[2] // RING
        return lax.dynamic_slice_in_dim(array[0], wrap(y + shift) * wide, wide, 1)

    weights = lax.all_gather(out_weight, ("zh", "zl", "x", "y"), axis=0, tiled=True)

    pieces, q_pieces = [], []
    for shift in SHIFTS:
        kv = jnp.concatenate([head_slice(keys, -shift), head_slice(values, -shift)], axis=1)
        pieces.append(kv if shift == 0 else shifted(kv, "y", -shift))
    for shift in SHIFTS:
        q = head_slice(query, -shift)
        q_pieces.append(q if shift == 0 else shifted(q, "y", -shift))
    own = jnp.stack(pieces)
    far = shifted(own, "zl", 1, 2)
    near = ring_gather(own, "x")
    opposite = jnp.concatenate([near[3], near[4]], axis=0)
    far_all = (far, shifted(far, "x", 1), shifted(far, "x", -1), shifted(opposite, "zl", 1, 2))
    attended = attention(table, SHIFTS, q_pieces, near + far_all, sec, nsec)

    by_shift = dict(zip(SHIFTS, attended))
    back = {0: by_shift[0]}
    for shift in SHIFTS[1:]:
        back[wrap_static(-shift)] = shifted(by_shift[shift], "y", shift)
    own_att = [back[s] for s in SHIFTS]
    other_att = [shifted(a, "c", 1, 2) for a in own_att]
    base = 2 * nsec
    whole, for_other = project(table, base, own_att, other_att, weights)
    return merge(table, base, shifted(for_other, "c", 1, 2), whole)[None]


def wrap_static(shift):
    return 2 if shift in (2, -2) else shift


def solution(mesh):
    fine = Mesh(mesh.devices.reshape(2, 2, 2, 4, 4), ("zh", "c", "zl", "x", "y"))
    dp, ctx = ("zh", "c"), ("zl", "x", "y")
    return jax.shard_map(
        per_device,
        mesh=fine,
        in_specs=(
            P(dp, ctx, None),
            P(dp, ctx, None),
            P(dp, ctx, None),
            P(),
            P(dp, None),
            P(dp, None),
            P(ctx, dp),
        ),
        out_specs=P(dp, ctx, None),
        check_vma=False,
    )
```

```python
import functools
import math

import jax
import jax.numpy as jnp
from jax import lax
from jax.experimental import pallas as pl
from jax.experimental.pallas import tpu as pltpu
from jax.sharding import Mesh, PartitionSpec as P

HD = 128
RING = 4
SHIFTS = (0, -1, 1, 2)
BLOCK_KEYS = 2048
TAIL_STEP = 256
ROW_TILE = 16


def shifted(array, axis, step, size=RING):
    return lax.ppermute(array, axis, [(i, (i + step) % size) for i in range(size)])


def ring_gather(array, axis):
    half = array.shape[0] // 2
    from_left = shifted(array, axis, 1)
    from_right = shifted(array, axis, -1)
    far_head = shifted(from_left[:half], axis, 1)
    far_tail = shifted(from_right[half:], axis, -1)
    return array, from_left, from_right, far_head, far_tail


def wrap(value):
    return lax.rem(value + RING, RING)


def attention_kernel(
    groups, sec, nsec, shifts, table, *refs
):
    count = len(shifts)
    q_refs, kv_refs, out_refs = refs[:count], refs[count : count + 9], refs[count + 9 : 2 * count + 9]
    held, q_all, out_all, acc, peak, sem = refs[2 * count + 9 :]
    base = 2 * nsec
    zl, x, y = table[base + 2], table[base + 3], table[base + 4]
    rows = nsec * sec
    factor = math.log2(math.e) / math.sqrt(HD)

    def copies(act):
        for side in range(2):
            own_zl = zl if side == 0 else 1 - zl
            for x_rel in range(4):
                abs_x = wrap(x + SHIFTS[x_rel])
                for y_rel in range(4):
                    abs_y = wrap(y + SHIFTS[y_rel])
                    if side == 1:
                        source = kv_refs[5 + x_rel].at[y_rel]
                    elif x_rel < 3:
                        source = kv_refs[x_rel].at[y_rel]
                    else:
                        source = kv_refs[3 + y_rel // 2].at[y_rel % 2]
                    for part in range(2):
                        section = ((own_zl * RING + abs_x) * RING + abs_y) * 2 + part
                        at = pl.multiple_of(table[section] * sec, ROW_TILE)
                        act(
                            source.at[pl.ds(part * sec, sec), :],
                            held.at[pl.ds(at, sec), pl.ds(0, 2 * HD)],
                        )

    copies(lambda a, b: pltpu.make_async_copy(a, b, sem).start())
    pad = held.shape[0] - rows
    held[pl.ds(rows, pad), pl.ds(0, 2 * HD)] = jnp.zeros((pad, 2 * HD), held.dtype)
    held[:, pl.ds(2 * HD, HD)] = jnp.ones((held.shape[0], HD), held.dtype)
    copies(lambda a, b: pltpu.make_async_copy(a, b, sem).wait())

    first, second = table[base], table[base + 1]

    def segment_start(pos):
        return jnp.where(pos >= second, second, jnp.where(pos >= first, first, 0))

    for piece in range(count):
        q_all[pl.ds(piece * 2 * sec, 2 * sec), :] = q_refs[piece][...]

    def one_section(index, _):
        piece, part = index // 2, lax.rem(index, 2)
        shift = shifts[0]
        for i in range(1, count):
            shift = jnp.where(piece == i, shifts[i], shift)
        section = ((zl * RING + x) * RING + wrap(y + shift)) * 2 + part
        place = table[section]
        begin = place * sec
        own_rows = pl.ds(pl.multiple_of(index * sec, ROW_TILE), sec)

        @pl.when(table[nsec + place] == 0)
        def _():
            out_all[own_rows, :] = jnp.zeros((sec, groups * HD), out_all.dtype)

        @pl.when(table[nsec + place] != 0)
        def _():
            key_first = segment_start(begin) // ROW_TILE * ROW_TILE
            last_start = segment_start(begin + sec - 1)
            full = (begin + sec - key_first) // BLOCK_KEYS
            tail_first = key_first + full * BLOCK_KEYS
            tail_steps = (begin + sec - tail_first + TAIL_STEP - 1) // TAIL_STEP
            peak[...] = jnp.full(peak.shape, -1e30, jnp.float32)
            acc[...] = jnp.zeros(acc.shape, jnp.float32)

            def step(first, width, masked):
                at = pl.multiple_of(first, ROW_TILE)
                keys = held[pl.ds(at, width), pl.ds(0, HD)]
                values = held[pl.ds(at, width), pl.ds(HD, 2 * HD)]
                if masked:
                    row_pos = begin + lax.broadcasted_iota(jnp.int32, (sec, 1), 0)
                    row_start = segment_start(row_pos)
                    key_pos = at + lax.broadcasted_iota(jnp.int32, (1, width), 1)
                    seen = (key_pos <= row_pos) & (key_pos >= row_start)
                def score(g):
                    got = lax.dot_general(
                        q_all[own_rows, pl.ds(g * HD, HD)],
                        keys,
                        (((1,), (1,)), ((), ())),
                        preferred_element_type=jnp.float32,
                    )
                    return jnp.where(seen, got, -1e30) if masked else got

                def weigh(g, got):
                    rows_g = pl.ds(g * sec, sec)
                    before = peak[rows_g, :]
                    top = jnp.maximum(before, jnp.max(got, axis=1, keepdims=True))
                    peak[rows_g, :] = top
                    scaled = top * factor
                    weights = jnp.exp2(
                        got * factor - jnp.concatenate([scaled] * (width // HD), axis=1)
                    ).astype(jnp.bfloat16)
                    return weights, jnp.exp2(before * factor - scaled)

                def add(g, weights, rescale):
                    rows_g = pl.ds(g * sec, sec)
                    acc[rows_g, :] = acc[rows_g, :] * jnp.concatenate(
                        [rescale, rescale], axis=1
                    ) + jnp.dot(weights, values, preferred_element_type=jnp.float32)

                ahead = score(0)
                waiting = None
                for g in range(groups):
                    got, ahead = ahead, score(g + 1) if g + 1 < groups else None
                    if waiting is not None:
                        add(g - 1, *waiting)
                    waiting = weigh(g, got)
                add(groups - 1, *waiting)

            def full_block(block, _):
                first = key_first + block * BLOCK_KEYS
                masked = (first < last_start) | (first + BLOCK_KEYS > begin)
                pl.when(masked)(lambda: step(first, BLOCK_KEYS, True))
                pl.when(jnp.logical_not(masked))(lambda: step(first, BLOCK_KEYS, False))
                return 0

            lax.fori_loop(0, full, full_block, 0)
            for steps in range(1, BLOCK_KEYS // TAIL_STEP + 1):
                pl.when(tail_steps == steps)(
                    lambda steps=steps: step(tail_first, steps * TAIL_STEP, True)
                )
            for g in range(groups):
                rows_g = pl.ds(g * sec, sec)
                out_all[own_rows, pl.ds(g * HD, HD)] = (
                    acc[rows_g, pl.ds(0, HD)] / acc[rows_g, pl.ds(HD, HD)]
                ).astype(out_all.dtype)

        return 0

    lax.fori_loop(0, 2 * count, one_section, 0)
    for piece in range(count):
        out_refs[piece][...] = out_all[pl.ds(piece * 2 * sec, 2 * sec), :]


def attention(table, shifts, q_pieces, kv_pieces, sec, nsec):
    groups = q_pieces[0].shape[1] // HD
    rows = nsec * sec
    count = len(shifts)
    smem = pl.BlockSpec(memory_space=pltpu.SMEM)
    vmem = pl.BlockSpec(memory_space=pltpu.VMEM)
    return pl.pallas_call(
        functools.partial(attention_kernel, groups, sec, nsec, shifts),
        out_shape=[jax.ShapeDtypeStruct(q.shape, q.dtype) for q in q_pieces],
        in_specs=[smem] + [vmem] * count + [pl.BlockSpec(memory_space=pl.ANY)] * 9,
        out_specs=[vmem] * count,
        scratch_shapes=[
            pltpu.VMEM((rows + TAIL_STEP, 3 * HD), jnp.bfloat16),
            pltpu.VMEM((2 * count * sec, groups * HD), jnp.bfloat16),
            pltpu.VMEM((2 * count * sec, groups * HD), jnp.bfloat16),
            pltpu.VMEM((groups * sec, 2 * HD), jnp.float32),
            pltpu.VMEM((groups * sec, HD), jnp.float32),
            pltpu.SemaphoreType.DMA,
        ],
        compiler_params=pltpu.CompilerParams(vmem_limit_bytes=24 * 2**20),
        cost_estimate=pl.CostEstimate(
            flops=count * 2 * 10**9,
            bytes_accessed=6 * 10**6,
            transcendentals=count * 4 * 10**6,
        ),
        name="attend",
    )(table, *q_pieces, *kv_pieces)


def project_kernel(base, table, *refs):
    att_refs, weights = refs[:8], refs[8]
    own_out, other_out, att = refs[9:]
    tok, wide = att_refs[0].shape

    @pl.when(pl.program_id(0) == 0)
    def _():
        for who in range(2):
            for j in range(4):
                head = wrap(table[base + 4] + SHIFTS[j])
                at = pl.multiple_of(head * wide, HD)
                att[pl.ds(who * tok, tok), pl.ds(at, wide)] = att_refs[4 * who + j][...]

    got = jnp.dot(att[...], weights[...], preferred_element_type=jnp.float32)
    got = got.astype(own_out.dtype)
    own_out[...] = got[:tok]
    other_out[0] = got[tok:]


def project(table, base, own_att, other_att, weights):
    tok, wide = own_att[0].shape
    rows, cols = RING * wide, weights.shape[1]
    piece = pl.BlockSpec((tok, wide), lambda i, *_: (0, 0))
    return pl.pallas_call(
        functools.partial(project_kernel, base),
        out_shape=[
            jax.ShapeDtypeStruct((tok, 4 * cols), jnp.bfloat16),
            jax.ShapeDtypeStruct((2, tok, cols), jnp.bfloat16),
        ],
        grid_spec=pltpu.PrefetchScalarGridSpec(
            num_scalar_prefetch=1,
            grid=(2,),
            in_specs=[piece] * 8 + [pl.BlockSpec((rows, cols), lambda i, *_: (i, 0))],
            out_specs=[
                pl.BlockSpec((tok, cols), lambda i, table: (0, i * 2 + table[base + 6])),
                pl.BlockSpec((1, tok, cols), lambda i, *_: (i, 0, 0)),
            ],
            scratch_shapes=[pltpu.VMEM((2 * tok, rows), jnp.bfloat16)],
        ),
        compiler_params=pltpu.CompilerParams(vmem_limit_bytes=48 * 2**20),
        cost_estimate=pl.CostEstimate(
            flops=6 * 10**9, bytes_accessed=18 * 10**6, transcendentals=0
        ),
        name="project",
    )(table, *own_att, *other_att, weights)


def merge_kernel(base, table, theirs, whole, out, sems):
    del whole
    cols = theirs.shape[2]

    def store(half):
        at = pl.multiple_of((half * 2 + 1 - table[base + 6]) * cols, HD)
        return pltpu.make_async_copy(theirs.at[half], out.at[:, pl.ds(at, cols)], sems.at[half])

    for half in range(2):
        store(half).start()
    for half in range(2):
        store(half).wait()


def merge(table, base, theirs, whole):
    anywhere = pl.BlockSpec(memory_space=pl.ANY)
    return pl.pallas_call(
        functools.partial(merge_kernel, base),
        out_shape=jax.ShapeDtypeStruct(whole.shape, whole.dtype),
        in_specs=[
            pl.BlockSpec(memory_space=pltpu.SMEM),
            pl.BlockSpec(memory_space=pltpu.VMEM),
            anywhere,
        ],
        out_specs=anywhere,
        scratch_shapes=[pltpu.SemaphoreType.DMA((2,))],
        input_output_aliases={2: 0},
        compiler_params=pltpu.CompilerParams(vmem_limit_bytes=8 * 2**20),
        cost_estimate=pl.CostEstimate(flops=0, bytes_accessed=3 * 10**6, transcendentals=0),
        name="merge",
    )(table, theirs, whole)


def per_device(query, keys, values, section_order, kept_sections, segment_ids, out_weight):
    tok = query.shape[1]
    sec = tok // 2
    nsec = section_order.shape[0]
    zh, core = lax.axis_index("zh"), lax.axis_index("c")
    zl, x, y = lax.axis_index("zl"), lax.axis_index("x"), lax.axis_index("y")
    first, second = jnp.sum(segment_ids[0] < 1), jnp.sum(segment_ids[0] < 2)
    scalars = jnp.stack([first, second, zl, x, y, zh * 2 + zl, core]).astype(jnp.int32)
    table = jnp.concatenate([section_order, kept_sections[0], scalars])

    def head_slice(array, shift):
        wide = array.shape[2] // RING
        return lax.dynamic_slice_in_dim(array[0], wrap(y + shift) * wide, wide, 1)

    weights = lax.all_gather(out_weight, ("zh", "zl", "x", "y"), axis=0, tiled=True)

    pieces, q_pieces = [], []
    for shift in SHIFTS:
        kv = jnp.concatenate([head_slice(keys, -shift), head_slice(values, -shift)], axis=1)
        pieces.append(kv if shift == 0 else shifted(kv, "y", -shift))
    for shift in SHIFTS:
        q = head_slice(query, -shift)
        q_pieces.append(q if shift == 0 else shifted(q, "y", -shift))
    own = jnp.stack(pieces)
    far = shifted(own, "zl", 1, 2)
    near = ring_gather(own, "x")
    opposite = jnp.concatenate([near[3], near[4]], axis=0)
    far_all = (far, shifted(far, "x", 1), shifted(far, "x", -1), shifted(opposite, "zl", 1, 2))
    attended = attention(table, SHIFTS, q_pieces, near + far_all, sec, nsec)

    by_shift = dict(zip(SHIFTS, attended))
    back = {0: by_shift[0]}
    for shift in SHIFTS[1:]:
        back[wrap_static(-shift)] = shifted(by_shift[shift], "y", shift)
    own_att = [back[s] for s in SHIFTS]
    other_att = [shifted(a, "c", 1, 2) for a in own_att]
    base = 2 * nsec
    whole, for_other = project(table, base, own_att, other_att, weights)
    return merge(table, base, shifted(for_other, "c", 1, 2), whole)[None]


def wrap_static(shift):
    return 2 if shift in (2, -2) else shift


def solution(mesh):
    fine = Mesh(mesh.devices.reshape(2, 2, 2, 4, 4), ("zh", "c", "zl", "x", "y"))
    dp, ctx = ("zh", "c"), ("zl", "x", "y")
    return jax.shard_map(
        per_device,
        mesh=fine,
        in_specs=(
            P(dp, ctx, None),
            P(dp, ctx, None),
            P(dp, ctx, None),
            P(),
            P(dp, None),
            P(dp, None),
            P(ctx, dp),
        ),
        out_specs=P(dp, ctx, None),
        check_vma=False,
    )
```

```python
import functools
import math

import jax
import jax.numpy as jnp
from jax import lax
from jax.experimental import pallas as pl
from jax.experimental.pallas import tpu as pltpu
from jax.sharding import Mesh, PartitionSpec as P

HD = 128
RING = 4
SHIFTS = (0, -1, 1, 2)
BLOCK_KEYS = 2048
TAIL_STEP = 256
ROW_TILE = 16


def shifted(array, axis, step, size=RING):
    return lax.ppermute(array, axis, [(i, (i + step) % size) for i in range(size)])


def ring_gather(array, axis):
    half = array.shape[0] // 2
    from_left = shifted(array, axis, 1)
    from_right = shifted(array, axis, -1)
    far_head = shifted(from_left[:half], axis, 1)
    far_tail = shifted(from_right[half:], axis, -1)
    return array, from_left, from_right, far_head, far_tail


def wrap(value):
    return lax.rem(value + RING, RING)


def attention_kernel(
    groups, sec, nsec, shifts, table, *refs
):
    count = len(shifts)
    q_refs, kv_refs, out_refs = refs[:count], refs[count : count + 9], refs[count + 9 : 2 * count + 9]
    held, q_all, out_all, acc, peak, sem = refs[2 * count + 9 :]
    base = 2 * nsec
    zl, x, y = table[base + 2], table[base + 3], table[base + 4]
    rows = nsec * sec
    factor = math.log2(math.e) / math.sqrt(HD)

    def copies(act):
        for side in range(2):
            own_zl = zl if side == 0 else 1 - zl
            for x_rel in range(4):
                abs_x = wrap(x + SHIFTS[x_rel])
                for y_rel in range(4):
                    abs_y = wrap(y + SHIFTS[y_rel])
                    if side == 1:
                        source = kv_refs[5 + x_rel].at[y_rel]
                    elif x_rel < 3:
                        source = kv_refs[x_rel].at[y_rel]
                    else:
                        source = kv_refs[3 + y_rel // 2].at[y_rel % 2]
                    for part in range(2):
                        section = ((own_zl * RING + abs_x) * RING + abs_y) * 2 + part
                        at = pl.multiple_of(table[section] * sec, ROW_TILE)
                        act(
                            source.at[pl.ds(part * sec, sec), :],
                            held.at[pl.ds(at, sec), pl.ds(0, 2 * HD)],
                        )

    copies(lambda a, b: pltpu.make_async_copy(a, b, sem).start())
    pad = held.shape[0] - rows
    held[pl.ds(rows, pad), pl.ds(0, 2 * HD)] = jnp.zeros((pad, 2 * HD), held.dtype)
    held[:, pl.ds(2 * HD, HD)] = jnp.ones((held.shape[0], HD), held.dtype)
    copies(lambda a, b: pltpu.make_async_copy(a, b, sem).wait())

    first, second = table[base], table[base + 1]

    def segment_start(pos):
        return jnp.where(pos >= second, second, jnp.where(pos >= first, first, 0))

    for piece in range(count):
        q_all[pl.ds(piece * 2 * sec, 2 * sec), :] = q_refs[piece][...]

    def one_section(index, _):
        piece, part = index // 2, lax.rem(index, 2)
        shift = shifts[0]
        for i in range(1, count):
            shift = jnp.where(piece == i, shifts[i], shift)
        section = ((zl * RING + x) * RING + wrap(y + shift)) * 2 + part
        place = table[section]
        begin = place * sec
        own_rows = pl.ds(pl.multiple_of(index * sec, ROW_TILE), sec)

        @pl.when(table[nsec + place] == 0)
        def _():
            out_all[own_rows, :] = jnp.zeros((sec, groups * HD), out_all.dtype)

        @pl.when(table[nsec + place] != 0)
        def _():
            key_first = segment_start(begin) // ROW_TILE * ROW_TILE
            last_start = segment_start(begin + sec - 1)
            full = (begin + sec - key_first) // BLOCK_KEYS
            tail_first = key_first + full * BLOCK_KEYS
            tail_steps = (begin + sec - tail_first + TAIL_STEP - 1) // TAIL_STEP
            peak[...] = jnp.full(peak.shape, -1e30, jnp.float32)
            acc[...] = jnp.zeros(acc.shape, jnp.float32)

            def step(first, width, masked):
                at = pl.multiple_of(first, ROW_TILE)
                keys = held[pl.ds(at, width), pl.ds(0, HD)]
                values = held[pl.ds(at, width), pl.ds(HD, 2 * HD)]
                if masked:
                    row_pos = begin + lax.broadcasted_iota(jnp.int32, (sec, 1), 0)
                    row_start = segment_start(row_pos)
                    key_pos = at + lax.broadcasted_iota(jnp.int32, (1, width), 1)
                    seen = (key_pos <= row_pos) & (key_pos >= row_start)
                def score(g):
                    got = lax.dot_general(
                        q_all[own_rows, pl.ds(g * HD, HD)],
                        keys,
                        (((1,), (1,)), ((), ())),
                        preferred_element_type=jnp.float32,
                    )
                    return jnp.where(seen, got, -1e30) if masked else got

                def weigh(g, got):
                    rows_g = pl.ds(g * sec, sec)
                    before = peak[rows_g, :]
                    top = jnp.maximum(before, jnp.max(got, axis=1, keepdims=True))
                    peak[rows_g, :] = top
                    scaled = top * factor
                    weights = jnp.exp2(
                        got * factor - jnp.concatenate([scaled] * (width // HD), axis=1)
                    ).astype(jnp.bfloat16)
                    return weights, jnp.exp2(before * factor - scaled)

                def add(g, weights, rescale):
                    rows_g = pl.ds(g * sec, sec)
                    acc[rows_g, :] = acc[rows_g, :] * jnp.concatenate(
                        [rescale, rescale], axis=1
                    ) + jnp.dot(weights, values, preferred_element_type=jnp.float32)

                ahead = score(0)
                waiting = None
                for g in range(groups):
                    got, ahead = ahead, score(g + 1) if g + 1 < groups else None
                    if waiting is not None:
                        add(g - 1, *waiting)
                    waiting = weigh(g, got)
                add(groups - 1, *waiting)

            def full_block(block, _):
                first = key_first + block * BLOCK_KEYS
                masked = (first < last_start) | (first + BLOCK_KEYS > begin)
                pl.when(masked)(lambda: step(first, BLOCK_KEYS, True))
                pl.when(jnp.logical_not(masked))(lambda: step(first, BLOCK_KEYS, False))
                return 0

            lax.fori_loop(0, full, full_block, 0)
            for steps in range(1, BLOCK_KEYS // TAIL_STEP + 1):
                pl.when(tail_steps == steps)(
                    lambda steps=steps: step(tail_first, steps * TAIL_STEP, True)
                )
            for g in range(groups):
                rows_g = pl.ds(g * sec, sec)
                out_all[own_rows, pl.ds(g * HD, HD)] = (
                    acc[rows_g, pl.ds(0, HD)] / acc[rows_g, pl.ds(HD, HD)]
                ).astype(out_all.dtype)

        return 0

    lax.fori_loop(0, 2 * count, one_section, 0)
    for piece in range(count):
        out_refs[piece][...] = out_all[pl.ds(piece * 2 * sec, 2 * sec), :]


def attention(table, shifts, q_pieces, kv_pieces, sec, nsec):
    groups = q_pieces[0].shape[1] // HD
    rows = nsec * sec
    count = len(shifts)
    smem = pl.BlockSpec(memory_space=pltpu.SMEM)
    vmem = pl.BlockSpec(memory_space=pltpu.VMEM)
    return pl.pallas_call(
        functools.partial(attention_kernel, groups, sec, nsec, shifts),
        out_shape=[jax.ShapeDtypeStruct(q.shape, q.dtype) for q in q_pieces],
        in_specs=[smem] + [vmem] * count + [pl.BlockSpec(memory_space=pl.ANY)] * 9,
        out_specs=[vmem] * count,
        scratch_shapes=[
            pltpu.VMEM((rows + TAIL_STEP, 3 * HD), jnp.bfloat16),
            pltpu.VMEM((2 * count * sec, groups * HD), jnp.bfloat16),
            pltpu.VMEM((2 * count * sec, groups * HD), jnp.bfloat16),
            pltpu.VMEM((groups * sec, 2 * HD), jnp.float32),
            pltpu.VMEM((groups * sec, HD), jnp.float32),
            pltpu.SemaphoreType.DMA,
        ],
        compiler_params=pltpu.CompilerParams(vmem_limit_bytes=24 * 2**20),
        cost_estimate=pl.CostEstimate(
            flops=count * 2 * 10**9,
            bytes_accessed=6 * 10**6,
            transcendentals=count * 4 * 10**6,
        ),
        name="attend",
    )(table, *q_pieces, *kv_pieces)


def project_kernel(base, table, *refs):
    att_refs, weights = refs[:8], refs[8]
    own_out, other_out, att, sem = refs[9:]
    tok, wide = att_refs[0].shape

    @pl.when(pl.program_id(0) == 0)
    def _():
        here = pl.multiple_of(table[base + 4] * wide, HD)
        own = pltpu.make_async_copy(att_refs[0], att.at[pl.ds(0, tok), pl.ds(here, wide)], sem)
        own.start()
        for i in range(1, 8):
            at = pl.multiple_of(wrap(table[base + 4] + SHIFTS[i % 4]) * wide, HD)
            att[pl.ds(i // 4 * tok, tok), pl.ds(at, wide)] = att_refs[i][...]
        own.wait()

    got = jnp.dot(att[...], weights[...], preferred_element_type=jnp.float32)
    got = got.astype(own_out.dtype)
    own_out[...] = got[:tok]
    other_out[0] = got[tok:]


def project(table, base, own_att, other_att, weights):
    tok, wide = own_att[0].shape
    rows, cols = RING * wide, weights.shape[1]
    piece = pl.BlockSpec((tok, wide), lambda i, *_: (0, 0))
    return pl.pallas_call(
        functools.partial(project_kernel, base),
        out_shape=[
            jax.ShapeDtypeStruct((tok, 4 * cols), jnp.bfloat16),
            jax.ShapeDtypeStruct((2, tok, cols), jnp.bfloat16),
        ],
        grid_spec=pltpu.PrefetchScalarGridSpec(
            num_scalar_prefetch=1,
            grid=(2,),
            in_specs=[pl.BlockSpec(memory_space=pl.ANY)]
            + [piece] * 7
            + [pl.BlockSpec((rows, cols), lambda i, *_: (i, 0))],
            out_specs=[
                pl.BlockSpec((tok, cols), lambda i, table: (0, i * 2 + table[base + 6])),
                pl.BlockSpec((1, tok, cols), lambda i, *_: (i, 0, 0)),
            ],
            scratch_shapes=[
                pltpu.VMEM((2 * tok, rows), jnp.bfloat16),
                pltpu.SemaphoreType.DMA,
            ],
        ),
        compiler_params=pltpu.CompilerParams(vmem_limit_bytes=48 * 2**20),
        cost_estimate=pl.CostEstimate(
            flops=6 * 10**9, bytes_accessed=18 * 10**6, transcendentals=0
        ),
        name="project",
    )(table, *own_att, *other_att, weights)


def merge_kernel(base, table, theirs, whole, out, sems):
    del whole
    cols = theirs.shape[2]

    def store(half):
        at = pl.multiple_of((half * 2 + 1 - table[base + 6]) * cols, HD)
        return pltpu.make_async_copy(theirs.at[half], out.at[:, pl.ds(at, cols)], sems.at[half])

    for half in range(2):
        store(half).start()
    for half in range(2):
        store(half).wait()


def merge(table, base, theirs, whole):
    anywhere = pl.BlockSpec(memory_space=pl.ANY)
    return pl.pallas_call(
        functools.partial(merge_kernel, base),
        out_shape=jax.ShapeDtypeStruct(whole.shape, whole.dtype),
        in_specs=[
            pl.BlockSpec(memory_space=pltpu.SMEM),
            pl.BlockSpec(memory_space=pltpu.VMEM),
            anywhere,
        ],
        out_specs=anywhere,
        scratch_shapes=[pltpu.SemaphoreType.DMA((2,))],
        input_output_aliases={2: 0},
        compiler_params=pltpu.CompilerParams(vmem_limit_bytes=8 * 2**20),
        cost_estimate=pl.CostEstimate(flops=0, bytes_accessed=3 * 10**6, transcendentals=0),
        name="merge",
    )(table, theirs, whole)


def per_device(query, keys, values, section_order, kept_sections, segment_ids, out_weight):
    tok = query.shape[1]
    sec = tok // 2
    nsec = section_order.shape[0]
    zh, core = lax.axis_index("zh"), lax.axis_index("c")
    zl, x, y = lax.axis_index("zl"), lax.axis_index("x"), lax.axis_index("y")
    first, second = jnp.sum(segment_ids[0] < 1), jnp.sum(segment_ids[0] < 2)
    scalars = jnp.stack([first, second, zl, x, y, zh * 2 + zl, core]).astype(jnp.int32)
    table = jnp.concatenate([section_order, kept_sections[0], scalars])

    def head_slice(array, shift):
        wide = array.shape[2] // RING
        return lax.dynamic_slice_in_dim(array[0], wrap(y + shift) * wide, wide, 1)

    weights = lax.all_gather(out_weight, ("zh", "zl", "x", "y"), axis=0, tiled=True)

    pieces, q_pieces = [], []
    for shift in SHIFTS:
        kv = jnp.concatenate([head_slice(keys, -shift), head_slice(values, -shift)], axis=1)
        pieces.append(kv if shift == 0 else shifted(kv, "y", -shift))
    for shift in SHIFTS:
        q = head_slice(query, -shift)
        q_pieces.append(q if shift == 0 else shifted(q, "y", -shift))
    own = jnp.stack(pieces)
    far = shifted(own, "zl", 1, 2)
    near = ring_gather(own, "x")
    opposite = jnp.concatenate([near[3], near[4]], axis=0)
    far_all = (far, shifted(far, "x", 1), shifted(far, "x", -1), shifted(opposite, "zl", 1, 2))
    attended = attention(table, SHIFTS, q_pieces, near + far_all, sec, nsec)

    by_shift = dict(zip(SHIFTS, attended))
    back = {0: by_shift[0]}
    for shift in SHIFTS[1:]:
        back[wrap_static(-shift)] = shifted(by_shift[shift], "y", shift)
    own_att = [back[s] for s in SHIFTS]
    other_att = [shifted(a, "c", 1, 2) for a in own_att]
    base = 2 * nsec
    whole, for_other = project(table, base, own_att, other_att, weights)
    return merge(table, base, shifted(for_other, "c", 1, 2), whole)[None]


def wrap_static(shift):
    return 2 if shift in (2, -2) else shift


def solution(mesh):
    fine = Mesh(mesh.devices.reshape(2, 2, 2, 4, 4), ("zh", "c", "zl", "x", "y"))
    dp, ctx = ("zh", "c"), ("zl", "x", "y")
    return jax.shard_map(
        per_device,
        mesh=fine,
        in_specs=(
            P(dp, ctx, None),
            P(dp, ctx, None),
            P(dp, ctx, None),
            P(),
            P(dp, None),
            P(dp, None),
            P(ctx, dp),
        ),
        out_specs=P(dp, ctx, None),
        check_vma=False,
    )
```
